32 devices in a mesh: groups: 2 (over y), chan: 4 (over z), rows: 4 (over x, core).
Axes of the slice: x: 2, y: 2, z: 4, core: 2. Of those that a mesh axis runs over, the one named last changes fastest.
Arguments:
- image_tile: bfloat16 [128, 128, 4096], P(('groups', 'rows'), None, 'chan'), parts along dimension 0, may hold values from -6 to 6
- block_links: int32 [16, 8], replicated, may hold values from 0 to 15, all different within a row
- fan_count: int32 [16], replicated, may hold values from 1 to 8, 64 in all
- conv_weight: bfloat16 [16, 8, 9, 256, 256], P('chan'), may hold values from -0.0625 to 0.0625
- conv_bias: float32 [4096], P('chan'), may hold values from -3 to 3
- group_weight: bfloat16 [32, 9, 128, 128], P('chan'), may hold values from -0.1875 to 0.1875
Outputs:
- layer_out: bfloat16 [128, 128, 4096], P(('groups', 'rows'), None, 'chan'), parts along dimension 0
The draws below stay inside these ranges and needn't reach their ends.
There are 2 independent parts, one for each index of `groups`. The reference program is written for one: setup_inputs(seed, part) draws one part's arguments, and reference() takes and returns one part's arrays. A program takes and returns all parts, laid end to end along the dimension named above; an argument that names none is the same for every part. Nothing has to cross between parts.
Inputs may be any that keep to these rules, and one draw needn't show every extreme that they name: `block_links`: each row lists 8 distinct blocks; every block is listed in some row. Only the first fan_count[o] entries of row o are used. `fan_count`: the counts sum to 64.
All inputs are finite; a program needn't handle non-finite values.
Results may differ from the reference program's by a relative error of at most 0.0038.
Values may be sent and summed in bfloat16 or wider, within the bound.
No kernel may reach another device: no remote copies, remote signals or barrier semaphores. Data moves between devices by JAX's collectives and lax.ppermute only.
A program may use at most 256 MiB of HBM per device.

```python
import math
import jax
import jax.numpy as jnp
import numpy as np
from jax import lax

NB = 16
BLOCK = 256
GROUP = 128
FAN = 8
IMG_W = 128
CH = 4096
NG = 32
IMG_H = 64


def block_levels(rng, shape, pieces, low, top_value):
    factor_of, own = 1.0, jax.random.fold_in(rng, 6)
    for dim, parts in pieces:
        heights = jnp.exp(jax.random.uniform(jax.random.fold_in(own, dim), (parts,), jnp.float32, low / len(pieces), top_value / len(pieces)))
        factor_of = factor_of * jnp.repeat(heights, shape[dim] // parts).reshape([-1 if axis == dim else 1 for axis in range(len(shape))])
    return factor_of


def different_ones(own_key, rows, number_of, top, lift):
    ranking = jax.random.permutation(jax.random.fold_in(own_key, 1), number_of)
    pull = ranking
    for power in range(3):
        pull = pull * pull // number_of
    pull = pull * lift // number_of
    chance = jax.random.randint(jax.random.fold_in(own_key, 2), (rows, number_of), 0, 4096) + pull
    fixed_rows = jax.random.permutation(jax.random.fold_in(own_key, 3), rows)[jnp.arange(number_of) % rows]
    chance = jnp.where(jnp.arange(rows)[:, None] == fixed_rows[None, :], 1 << 14, chance)
    merit = chance * number_of + jnp.arange(number_of)
    return lax.top_k(merit.astype(jnp.int32), top)[1].astype(jnp.int32)


def profile(count, total, most, slope):
    loads = [(1 << 20) // math.isqrt(rank ** slope) + 1 for rank in range(2, count + 1)]
    surplus, holding = total - most - (count - 1), [1] * (count - 1)
    while surplus > 0:
        candidates = [i for i in range(count - 1) if holding[i] < most]
        mass, left = sum([loads[i] for i in candidates]), surplus
        for i in candidates:
            more = min(most - holding[i], max(1, left * loads[i] // mass), surplus)
            holding[i] = holding[i] + more
            surplus = surplus - more
    return np.array([most] + holding)


def uneven_parts(own_key, amount, total, bound, skew):
    if amount == 2:
        one = jax.random.randint(own_key, (), max(1, total - bound), min(bound, total - 1) + 1)
        return jnp.stack([one, total - one])
    lengths = jnp.asarray(profile(amount, total, bound, skew), jnp.int32)
    twos = (amount - 1) // 2
    source_of, sink = lengths[1:1 + 2 * twos:2], lengths[2:2 + 2 * twos:2]
    room = jnp.minimum(source_of - 1, bound - sink)
    passed = jax.random.randint(jax.random.fold_in(own_key, 1), (twos,), 0, 1 << 20) % (room + 1)
    lengths = lengths.at[1:1 + 2 * twos:2].set(source_of - passed).at[2:2 + 2 * twos:2].set(sink + passed)
    return lengths[jax.random.permutation(jax.random.fold_in(own_key, 2), amount)]


def scatter_about(stream_key, shape, scale, reach, split=(), kind=jnp.bfloat16):
    values = scale * jax.random.normal(stream_key, shape, jnp.float32)
    if split:
        values = values * block_levels(stream_key, shape, split, -0.22, 0.18)
    return jnp.clip(values, -reach, reach).astype(kind)


def setup_inputs(seed: int = 0, part: int = 0) -> dict:
    streams_of = jax.random.split(jax.random.key(seed), 7)
    part_splits = jax.random.split(jax.random.fold_in(streams_of[6], part), 7)
    image_tile = scatter_about(part_splits[0], (IMG_H, IMG_W, CH), 1.0, 6.0, ((0, 4), (2, 4)))
    block_links = different_ones(streams_of[1], NB, NB, FAN, 0)
    fan_count = uneven_parts(streams_of[2], NB, 4 * NB, FAN, 2).astype(jnp.int32)
    conv_weight = scatter_about(streams_of[3], (NB, FAN, 9, BLOCK, BLOCK), (9 * BLOCK * 4) ** -0.5, 0.0625, ((0, 4),))
    conv_bias = scatter_about(streams_of[4], (CH,), 0.5, 3.0, ((0, 4),), jnp.float32)
    group_weight = scatter_about(streams_of[5], (NG, 9, GROUP, GROUP), (9 * GROUP) ** -0.5, 0.1875, ((0, 4),))
    return {"image_tile": image_tile, "block_links": block_links, "fan_count": fan_count, "conv_weight": conv_weight, "conv_bias": conv_bias, "group_weight": group_weight}


def reference(image_tile, block_links, fan_count, conv_weight, conv_bias, group_weight):
    rows_all = image_tile.shape[0]
    cols_all = image_tile.shape[1]

    def one_block(target):
        def add_slot(slot_pos, running):
            source_block = block_links[target, slot_pos]
            chosen = lax.dynamic_slice_in_dim(image_tile, source_block * BLOCK, BLOCK, 2).astype(jnp.float32)
            kernel = conv_weight[target, slot_pos].astype(jnp.float32).reshape(3, 3, BLOCK, BLOCK)
            product = lax.conv_general_dilated(chosen[None], kernel, (1, 1), ((1, 1), (1, 1)),
                                               dimension_numbers=("NHWC", "HWIO", "NHWC"),
                                               precision=lax.Precision.HIGHEST)
            return running + product[0]
        start_sum = jnp.zeros((rows_all, cols_all, BLOCK), jnp.float32)
        return lax.fori_loop(0, fan_count[target], add_slot, start_sum)

    summed = lax.map(one_block, jnp.arange(NB, dtype=jnp.int32))
    summed = summed.transpose(1, 2, 0, 3).reshape(rows_all, cols_all, NB * BLOCK)
    hidden = jnp.maximum(summed + conv_bias.astype(jnp.float32), 0.0).astype(jnp.bfloat16)
    kernel_two = group_weight.astype(jnp.float32).reshape(NG, 3, 3, GROUP, GROUP)
    kernel_two = kernel_two.transpose(1, 2, 3, 0, 4).reshape(3, 3, GROUP, NG * GROUP)
    branch = lax.conv_general_dilated(hidden.astype(jnp.float32)[None], kernel_two, (1, 1), ((2, 2), (2, 2)),
                                      rhs_dilation=(2, 2),
                                      dimension_numbers=("NHWC", "HWIO", "NHWC"),
                                      feature_group_count=NG,
                                      precision=lax.Precision.HIGHEST)
    return (image_tile.astype(jnp.float32) + branch[0]).astype(jnp.bfloat16)
```

```python
import functools

import jax
import jax.numpy as jnp
from jax import lax
from jax.experimental import pallas as pl
from jax.experimental.pallas import tpu as pltpu
from jax.sharding import PartitionSpec as P

LANES = 128
VMEM_BYTES = 48 << 20


def lag_of(own):
    return 2 if own >= 2 else 1


def most_rounds(chans, own):
    lag = lag_of(own)
    return max(hop * lag + (chans - 1 - hop) * own for hop in range(chans - 1))


def plan_kernel(chans, own, rounds, links_ref, fans_ref, pick_ref, slot_ref):
    blocks, fan = links_ref.shape
    lag = lag_of(own)
    lane = lax.broadcasted_iota(jnp.int32, (blocks, LANES), 1)
    links = links_ref[...]
    fans = fans_ref[...]
    slot = jnp.full((blocks, LANES), -1, jnp.int32)
    for s in range(fan):
        slot = jnp.where((links[:, s : s + 1] == lane) & (fans > s), s, slot)
    slot_ref[...] = slot
    used = jnp.where(slot >= 0, 1.0, 0.0)
    far = jnp.full((1, LANES), -1.0, jnp.float32)
    near = jnp.full((1, LANES), float(chans), jnp.float32)
    for z in range(chans):
        up = jnp.max(used[z * own : (z + 1) * own], axis=0, keepdims=True)
        far = jnp.where(up > 0, float(z), far)
        w = chans - 1 - z
        down = jnp.max(used[w * own : (w + 1) * own], axis=0, keepdims=True)
        near = jnp.where(down > 0, float(w), near)
    shape = (2 * chans, LANES)
    row = lax.broadcasted_iota(jnp.int32, shape, 0)
    block = lax.broadcasted_iota(jnp.int32, shape, 1)
    mirrored = row >= chans
    here = jnp.where(mirrored, row - chans, row).astype(jnp.float32)
    home = jnp.zeros(shape, jnp.float32)
    for z in range(1, chans):
        home = home + jnp.where(block >= z * own, 1.0, 0.0)
    home = jnp.where(mirrored, chans - 1.0 - home, home)
    reach = jnp.where(mirrored, chans - 1.0 - near, far)
    blockf = block.astype(jnp.float32)
    left = jnp.where((reach > here) & (home <= here) & (block < blocks), 1.0, 0.0)
    held = jnp.where(home == here, 1.0, 0.0)
    rank = reach * 4096.0 + home * 128.0 + blockf
    sent = []
    for k in range(rounds):
        if k >= lag:
            held = jnp.maximum(held, pltpu.roll(sent[k - lag], 1, 0))
        score = jnp.where((left > 0) & (held > 0), rank, -1.0)
        best = jnp.max(score, axis=1, keepdims=True)
        chosen = jnp.where((score == best) & (best >= 0), 1.0, 0.0)
        sent.append(chosen)
        left = left - chosen
        which = jnp.max(jnp.where(chosen > 0, blockf, -1.0), axis=1, keepdims=True)
        pick_ref[k] = jnp.broadcast_to(which, shape).astype(jnp.int32)


def make_plan(block_links, fan_count, chans, own, rounds):
    blocks = block_links.shape[0]
    return pl.pallas_call(
        functools.partial(plan_kernel, chans, own, rounds),
        out_shape=(
            jax.ShapeDtypeStruct((rounds, 2 * chans, LANES), jnp.int32),
            jax.ShapeDtypeStruct((blocks, LANES), jnp.int32),
        ),
        name="plan",
    )(block_links, fan_count.reshape(blocks, 1))


def choose_kernel(k, own, size, me_ref, table_ref, image_ref, *refs):
    held = (len(refs) - 4) // 2
    from_left, from_right = refs[:held], refs[held : 2 * held]
    right_ref, left_ref, sems, _ = refs[2 * held :]
    base = me_ref[0] * own
    for d, (out_ref, got) in enumerate(((right_ref, from_left), (left_ref, from_right))):
        block = table_ref[4 * k + d]
        mine = (block >= base) & (block < base + own)

        @pl.when(mine)
        def _(d=d, out_ref=out_ref, block=block):
            start = pl.multiple_of((block - base) * size, size)
            pltpu.make_async_copy(image_ref.at[:, :, pl.ds(start, size)], out_ref, sems.at[d]).start()

        for j in range(held):
            same = (block >= 0) & jnp.logical_not(mine) & (table_ref[4 * j + 2 + d] == block)

            @pl.when(same)
            def _(d=d, out_ref=out_ref, ref=got[j]):
                pltpu.make_async_copy(ref, out_ref, sems.at[d]).start()

    for d, out_ref in enumerate((right_ref, left_ref)):

        @pl.when(table_ref[4 * k + d] >= 0)
        def _(d=d, out_ref=out_ref):
            pltpu.make_async_copy(image_ref.at[:, :, pl.ds(0, size)], out_ref, sems.at[d]).wait()


def choose(k, own, size, me, table, image, from_left, from_right):
    rows, cols, _ = image.shape
    shape = jax.ShapeDtypeStruct((rows, cols, size), image.dtype)
    anywhere = pl.BlockSpec(memory_space=pl.ANY)
    scalars = pl.BlockSpec(memory_space=pltpu.SMEM)
    return pl.pallas_call(
        functools.partial(choose_kernel, k, own, size),
        out_shape=(shape, shape),
        in_specs=[scalars, scalars] + [anywhere] * (1 + len(from_left) + len(from_right)),
        out_specs=(anywhere, anywhere),
        scratch_shapes=[pltpu.SemaphoreType.DMA((2,)), pltpu.SMEM((1,), jnp.int32)],
        cost_estimate=pl.CostEstimate(flops=0, bytes_accessed=4 * rows * cols * size * 2, transcendentals=0),
        name=f"choose_{k}",
    )(me, table, image, *from_left, *from_right)


def shifted(y, step, col):
    cols = y.shape[1]
    moved = pltpu.roll(y, step % cols, 1)
    return jnp.where((col >= step) & (col < cols + step), moved, 0.0)


def stencil(xe_ref, weight_of, rows, cols, gap, add):
    step = 4
    width = xe_ref.shape[2]
    col = lax.broadcasted_iota(jnp.int32, (step, cols, 1), 1)
    for r in range(0, rows, step):
        wide = jnp.concatenate(
            [xe_ref[r + a * gap : r + a * gap + step].reshape(step * cols, width) for a in range(3)], axis=1
        )
        total = None
        for c in range(3):
            y = jnp.dot(wide, weight_of(c), preferred_element_type=jnp.float32)
            y = y.reshape(step, cols, y.shape[-1])
            if c != 1:
                y = shifted(y, (1 - c) * gap, col)
            total = y if total is None else total + y
        add(r, total)


def taps_of(weight_ref):
    size = weight_ref.shape[-2]

    def weight_of(c):
        return jnp.concatenate([weight_ref[0, 0, 3 * a + c] for a in range(3)], axis=0)

    return weight_of


def own_kernel(slots_ref, x_ref, top_ref, bottom_ref, weight_ref, sums_ref, xe_ref):
    o, i = pl.program_id(0), pl.program_id(1)
    rows, cols, _ = x_ref.shape

    @pl.when(i == 0)
    def _():
        sums_ref[...] = jnp.zeros_like(sums_ref)

    @pl.when(slots_ref[o * pl.num_programs(1) + i] >= 0)
    def _():
        xe_ref[1 : rows + 1] = x_ref[...]
        xe_ref[0:1] = top_ref[...]
        xe_ref[rows + 1 : rows + 2] = bottom_ref[...]

        def add(r, total):
            n = total.shape[0]
            sums_ref[0, r : r + n] += total

        stencil(xe_ref, taps_of(weight_ref), rows, cols, 1, add)


def own_sums(slots, image, top, bottom, conv_weight):
    rows, cols, chans = image.shape
    outs, _, taps, size, _ = conv_weight.shape
    own = chans // size
    return pl.pallas_call(
        own_kernel,
        out_shape=jax.ShapeDtypeStruct((outs, rows, cols, size), jnp.float32),
        grid_spec=pltpu.PrefetchScalarGridSpec(
            num_scalar_prefetch=1,
            grid=(outs, own),
            in_specs=[
                pl.BlockSpec((rows, cols, size), lambda o, i, s: (0, 0, i)),
                pl.BlockSpec((1, cols, size), lambda o, i, s: (0, 0, i)),
                pl.BlockSpec((1, cols, size), lambda o, i, s: (0, 0, i)),
                pl.BlockSpec(
                    (1, 1, taps, size, size),
                    lambda o, i, s: (o, jnp.maximum(s[o * own + i], 0), 0, 0, 0),
                ),
            ],
            out_specs=pl.BlockSpec((1, rows, cols, size), lambda o, i, s: (o, 0, 0, 0)),
            scratch_shapes=[pltpu.VMEM((rows + 2, cols, size), jnp.bfloat16)],
        ),
        compiler_params=pltpu.CompilerParams(vmem_limit_bytes=VMEM_BYTES),
        cost_estimate=pl.CostEstimate(
            flops=outs * 2 * taps * rows * cols * size * size, bytes_accessed=30 << 20, transcendentals=0
        ),
        name="own_sums",
    )(slots, image, top, bottom, conv_weight)


def more_kernel(final, slots_ref, one_ref, two_ref, top_ref, bottom_ref, weight_ref, before_ref, *refs):
    if final:
        bias_ref, out_ref, xe_ref, sums_ref = refs
    else:
        sums_ref, xe_ref = refs
    o, d = pl.program_id(0), pl.program_id(1)
    rows, cols, _ = one_ref.shape

    @pl.when(d == 0)
    def _():
        sums_ref[...] = before_ref[...]

    wanted = slots_ref[2 * o + d] >= 0
    for side, x_ref in enumerate((one_ref, two_ref)):

        @pl.when(wanted & (d == side))
        def _(side=side, x_ref=x_ref):
            xe_ref[1 : rows + 1] = x_ref[...]
            xe_ref[0:1] = top_ref[side : side + 1]
            xe_ref[rows + 1 : rows + 2] = bottom_ref[side : side + 1]

    @pl.when(wanted)
    def _():
        def add(r, total):
            n = total.shape[0]
            sums_ref[0, r : r + n] += total

        stencil(xe_ref, taps_of(weight_ref), rows, cols, 1, add)

    if final:

        @pl.when(d == 1)
        def _():
            out_ref[...] = jnp.maximum(sums_ref[0] + bias_ref[...].reshape(1, 1, -1), 0.0).astype(out_ref.dtype)


def more_sums(slots, one, two, top, bottom, conv_weight, sums, bias=None):
    rows, cols, size = one.shape
    outs, _, taps, _, _ = conv_weight.shape
    final = bias is not None
    whole = lambda o, d, s: (0, 0, 0)
    at_out = lambda o, d, s: (o, 0, 0, 0)
    in_specs = [
        pl.BlockSpec((rows, cols, size), whole),
        pl.BlockSpec((rows, cols, size), whole),
        pl.BlockSpec((2, cols, size), whole),
        pl.BlockSpec((2, cols, size), whole),
        pl.BlockSpec((1, 1, taps, size, size), lambda o, d, s: (o, jnp.maximum(s[2 * o + d], 0), 0, 0, 0)),
        pl.BlockSpec((1, rows, cols, size), at_out),
    ]
    args = [slots, one, two, top, bottom, conv_weight, sums]
    scratch = [pltpu.VMEM((rows + 2, cols, size), jnp.bfloat16)]
    if final:
        in_specs.append(pl.BlockSpec((1, size), lambda o, d, s: (0, o)))
        args.append(bias)
        out_shape = jax.ShapeDtypeStruct((rows, cols, outs * size), jnp.bfloat16)
        out_spec = pl.BlockSpec((rows, cols, size), lambda o, d, s: (0, 0, o))
        scratch.append(pltpu.VMEM((1, rows, cols, size), jnp.float32))
        alias = {}
    else:
        out_shape = jax.ShapeDtypeStruct(sums.shape, sums.dtype)
        out_spec = pl.BlockSpec((1, rows, cols, size), at_out)
        alias = {6: 0}
    return pl.pallas_call(
        functools.partial(more_kernel, final),
        out_shape=out_shape,
        grid_spec=pltpu.PrefetchScalarGridSpec(
            num_scalar_prefetch=1, grid=(outs, 2), in_specs=in_specs, out_specs=out_spec, scratch_shapes=scratch
        ),
        input_output_aliases=alias,
        compiler_params=pltpu.CompilerParams(vmem_limit_bytes=VMEM_BYTES),
        cost_estimate=pl.CostEstimate(
            flops=3 * 2 * taps * rows * cols * size * size, bytes_accessed=26 << 20, transcendentals=0
        ),
        name="last_sums" if final else "more_sums",
    )(*args)


def branch_kernel(x_ref, top_ref, bottom_ref, image_ref, weight_ref, out_ref, xe_ref):
    rows, cols, _ = x_ref.shape
    xe_ref[0:2] = top_ref[...]
    xe_ref[2 : rows + 2] = x_ref[...]
    xe_ref[rows + 2 : rows + 4] = bottom_ref[...]

    def add(r, total):
        n = total.shape[0]
        out_ref[r : r + n] = (image_ref[r : r + n].astype(jnp.float32) + total).astype(out_ref.dtype)

    stencil(xe_ref, lambda c: weight_ref[0, c], rows, cols, 2, add)


def branch_out(hidden, top, bottom, image, paired):
    rows, cols, chans = image.shape
    pairs, _, deep, size = paired.shape
    block = lambda n: pl.BlockSpec((n, cols, size), lambda o: (0, 0, o))
    return pl.pallas_call(
        branch_kernel,
        out_shape=jax.ShapeDtypeStruct(image.shape, image.dtype),
        grid=(pairs,),
        in_specs=[
            block(rows),
            block(2),
            block(2),
            block(rows),
            pl.BlockSpec((1, 3, deep, size), lambda o: (o, 0, 0, 0)),
        ],
        out_specs=block(rows),
        scratch_shapes=[pltpu.VMEM((rows + 4, cols, size), jnp.bfloat16)],
        compiler_params=pltpu.CompilerParams(vmem_limit_bytes=VMEM_BYTES),
        cost_estimate=pl.CostEstimate(
            flops=2 * 3 * pairs * deep * size * rows * cols, bytes_accessed=18 << 20, transcendentals=0
        ),
        name="branch_out",
    )(hidden, top, bottom, image, paired)


def pair_weights(group_weight):
    groups, taps, g, _ = group_weight.shape
    w = group_weight.reshape(groups // 2, 2, 3, 3, g, g)
    zero = jnp.zeros_like(w[:, 0])
    upper = jnp.concatenate([w[:, 0], zero], axis=-1)
    lower = jnp.concatenate([zero, w[:, 1]], axis=-1)
    both = jnp.concatenate([upper, lower], axis=-2)
    return both.transpose(0, 2, 1, 3, 4).reshape(groups // 2, 3, 3 * 2 * g, 2 * g)


def along_rows(upper, lower):
    n = lax.axis_size("rows")
    down = [(i, i + 1) for i in range(n - 1)]
    up = [(i + 1, i) for i in range(n - 1)]
    return lax.ppermute(upper, "rows", down), lax.ppermute(lower, "rows", up)


def shards(image, block_links, fan_count, conv_weight, conv_bias, group_weight):
    rows, cols, _ = image.shape
    outs, fan, taps, size, _ = conv_weight.shape
    own = image.shape[2] // size
    blocks = block_links.shape[0]
    chans = lax.axis_size("chan")
    z = lax.axis_index("chan")
    most = most_rounds(chans, own)
    lag = lag_of(own)

    picks, slot_of = make_plan(block_links, fan_count, chans, own, most)
    picks = picks[:, :, 0]
    rounds = jnp.sum(jnp.any(picks >= 0, axis=1).astype(jnp.int32))
    padded = jnp.pad(picks, ((0, 0), (1, 1)), constant_values=-1)
    mirror = chans + chans - 1 - z
    at = lambda r: lax.dynamic_slice_in_dim(padded, r + 1, 1, 1)
    nothing = jnp.full((most, 1), -1, jnp.int32)
    got_left = jnp.where(z > 0, at(z - 1), nothing)
    got_right = jnp.where(z < chans - 1, at(mirror - 1), nothing)
    table = jnp.concatenate([at(z), at(mirror), got_left, got_right], axis=1)
    my_slots = lax.dynamic_slice_in_dim(slot_of, z * outs, outs, 0)[:, :blocks]
    own_slots = lax.dynamic_slice_in_dim(my_slots, z * own, own, 1).reshape(-1)
    arrived = table[:, 2:]
    hit = arrived[:, None, :, None] == jnp.arange(blocks, dtype=jnp.int32)
    more_slots = jnp.max(jnp.where(hit, my_slots[None, :, None, :], -1), axis=-1).reshape(most, outs * 2)
    me = z.reshape(1)
    table = table.reshape(-1)
    paired = pair_weights(group_weight)
    bias = conv_bias.reshape(1, -1)
    right = [(i, i + 1) for i in range(chans - 1)]
    left = [(i + 1, i) for i in range(chans - 1)]

    def run(count):
        from_left, from_right, sums = [], [], None
        hidden = None
        for k in range(count):
            ready = max(k - lag + 1, 0)
            out_right, out_left = choose(
                k, own, size, me, table, image, from_left[:ready], from_right[:ready]
            )
            from_left.append(lax.ppermute(out_right, "chan", right))
            from_right.append(lax.ppermute(out_left, "chan", left))
        top, bottom = along_rows(image[rows - 1 :], image[:1])
        sums = own_sums(own_slots, image, top, bottom, conv_weight)
        for k in range(count):
            one, two = from_left[k], from_right[k]
            top, bottom = along_rows(
                jnp.concatenate([one[rows - 1 :], two[rows - 1 :]], axis=0),
                jnp.concatenate([one[:1], two[:1]], axis=0),
            )
            last = bias if k == count - 1 else None
            sums = more_sums(more_slots[k], one, two, top, bottom, conv_weight, sums, last)
        hidden = sums
        top, bottom = along_rows(hidden[rows - 2 :], hidden[:2])
        return branch_out(hidden, top, bottom, image, paired)

    choices = list(range(blocks // 2, most + 1)) if chans <= 4 else [most]
    if len(choices) == 1:
        return run(choices[0])
    branch = jnp.clip(rounds - choices[0], 0, len(choices) - 1)
    return lax.switch(branch, [functools.partial(run, n) for n in choices])


def solution(mesh):
    in_specs = (
        P(("groups", "rows"), None, "chan"),
        P(),
        P(),
        P("chan", None, None, None, None),
        P("chan"),
        P("chan", None, None, None),
    )
    out_specs = P(("groups", "rows"), None, "chan")
    return jax.shard_map(shards, mesh=mesh, in_specs=in_specs, out_specs=out_specs, check_vma=False)
```

```python
import functools

import jax
import jax.numpy as jnp
from jax import lax
from jax.experimental import pallas as pl
from jax.experimental.pallas import tpu as pltpu
from jax.sharding import PartitionSpec as P

LANES = 128
VMEM_BYTES = 48 << 20


def lag_of(own):
    return 2 if own >= 2 else 1


def most_rounds(chans, own):
    lag = lag_of(own)
    return max(hop * lag + (chans - 1 - hop) * own for hop in range(chans - 1))


def plan_kernel(chans, own, rounds, links_ref, fans_ref, pick_ref, slot_ref):
    blocks, fan = links_ref.shape
    lag = lag_of(own)
    lane = lax.broadcasted_iota(jnp.int32, (blocks, LANES), 1)
    links = links_ref[...]
    fans = fans_ref[...]
    slot = jnp.full((blocks, LANES), -1, jnp.int32)
    for s in range(fan):
        slot = jnp.where((links[:, s : s + 1] == lane) & (fans > s), s, slot)
    slot_ref[...] = slot
    used = jnp.where(slot >= 0, 1.0, 0.0)
    far = jnp.full((1, LANES), -1.0, jnp.float32)
    near = jnp.full((1, LANES), float(chans), jnp.float32)
    for z in range(chans):
        up = jnp.max(used[z * own : (z + 1) * own], axis=0, keepdims=True)
        far = jnp.where(up > 0, float(z), far)
        w = chans - 1 - z
        down = jnp.max(used[w * own : (w + 1) * own], axis=0, keepdims=True)
        near = jnp.where(down > 0, float(w), near)
    shape = (2 * chans, LANES)
    row = lax.broadcasted_iota(jnp.int32, shape, 0)
    block = lax.broadcasted_iota(jnp.int32, shape, 1)
    mirrored = row >= chans
    here = jnp.where(mirrored, row - chans, row).astype(jnp.float32)
    home = jnp.zeros(shape, jnp.float32)
    for z in range(1, chans):
        home = home + jnp.where(block >= z * own, 1.0, 0.0)
    home = jnp.where(mirrored, chans - 1.0 - home, home)
    reach = jnp.where(mirrored, chans - 1.0 - near, far)
    blockf = block.astype(jnp.float32)
    left = jnp.where((reach > here) & (home <= here) & (block < blocks), 1.0, 0.0)
    held = jnp.where(home == here, 1.0, 0.0)
    rank = reach * 4096.0 + home * 128.0 + blockf
    sent = []
    for k in range(rounds):
        if k >= lag:
            held = jnp.maximum(held, pltpu.roll(sent[k - lag], 1, 0))
        score = jnp.where((left > 0) & (held > 0), rank, -1.0)
        best = jnp.max(score, axis=1, keepdims=True)
        chosen = jnp.where((score == best) & (best >= 0), 1.0, 0.0)
        sent.append(chosen)
        left = left - chosen
        which = jnp.max(jnp.where(chosen > 0, blockf, -1.0), axis=1, keepdims=True)
        pick_ref[k] = jnp.broadcast_to(which, shape).astype(jnp.int32)


def make_plan(block_links, fan_count, chans, own, rounds):
    blocks = block_links.shape[0]
    return pl.pallas_call(
        functools.partial(plan_kernel, chans, own, rounds),
        out_shape=(
            jax.ShapeDtypeStruct((rounds, 2 * chans, LANES), jnp.int32),
            jax.ShapeDtypeStruct((blocks, LANES), jnp.int32),
        ),
        name="plan",
    )(block_links, fan_count.reshape(blocks, 1))


def choose_kernel(k, own, size, me_ref, table_ref, image_ref, *refs):
    held = (len(refs) - 4) // 2
    from_left, from_right = refs[:held], refs[held : 2 * held]
    right_ref, left_ref, sems, _ = refs[2 * held :]
    base = me_ref[0] * own
    for d, (out_ref, got) in enumerate(((right_ref, from_left), (left_ref, from_right))):
        block = table_ref[4 * k + d]
        mine = (block >= base) & (block < base + own)

        @pl.when(mine)
        def _(d=d, out_ref=out_ref, block=block):
            start = pl.multiple_of((block - base) * size, size)
            pltpu.make_async_copy(image_ref.at[:, :, pl.ds(start, size)], out_ref, sems.at[d]).start()

        for j in range(held):
            same = (block >= 0) & jnp.logical_not(mine) & (table_ref[4 * j + 2 + d] == block)

            @pl.when(same)
            def _(d=d, out_ref=out_ref, ref=got[j]):
                pltpu.make_async_copy(ref, out_ref, sems.at[d]).start()

    for d, out_ref in enumerate((right_ref, left_ref)):

        @pl.when(table_ref[4 * k + d] >= 0)
        def _(d=d, out_ref=out_ref):
            pltpu.make_async_copy(image_ref.at[:, :, pl.ds(0, size)], out_ref, sems.at[d]).wait()


def choose(k, own, size, me, table, image, from_left, from_right):
    rows, cols, _ = image.shape
    shape = jax.ShapeDtypeStruct((rows, cols, size), image.dtype)
    anywhere = pl.BlockSpec(memory_space=pl.ANY)
    scalars = pl.BlockSpec(memory_space=pltpu.SMEM)
    return pl.pallas_call(
        functools.partial(choose_kernel, k, own, size),
        out_shape=(shape, shape),
        in_specs=[scalars, scalars] + [anywhere] * (1 + len(from_left) + len(from_right)),
        out_specs=(pl.BlockSpec(memory_space=pltpu.VMEM),) * 2,
        scratch_shapes=[pltpu.SemaphoreType.DMA((2,)), pltpu.SMEM((1,), jnp.int32)],
        compiler_params=pltpu.CompilerParams(vmem_limit_bytes=VMEM_BYTES),
        cost_estimate=pl.CostEstimate(flops=0, bytes_accessed=4 * rows * cols * size * 2, transcendentals=0),
        name=f"choose_{k}",
    )(me, table, image, *from_left, *from_right)


def shifted(y, step, col):
    cols = y.shape[1]
    moved = pltpu.roll(y, step % cols, 1)
    return jnp.where((col >= step) & (col < cols + step), moved, 0.0)


def stencil(xe_ref, weight_of, rows, cols, gap, add):
    step = 4
    width = xe_ref.shape[2]
    col = lax.broadcasted_iota(jnp.int32, (step, cols, 1), 1)
    for r in range(0, rows, step):
        wide = jnp.concatenate(
            [xe_ref[r + a * gap : r + a * gap + step].reshape(step * cols, width) for a in range(3)], axis=1
        )
        total = None
        for c in range(3):
            y = jnp.dot(wide, weight_of(c), preferred_element_type=jnp.float32)
            y = y.reshape(step, cols, y.shape[-1])
            if c != 1:
                y = shifted(y, (1 - c) * gap, col)
            total = y if total is None else total + y
        add(r, total)


def taps_of(weight_ref):
    size = weight_ref.shape[-2]

    def weight_of(c):
        return jnp.concatenate([weight_ref[0, 0, 3 * a + c] for a in range(3)], axis=0)

    return weight_of


def own_kernel(slots_ref, x_ref, top_ref, bottom_ref, weight_ref, sums_ref, xe_ref):
    o, i = pl.program_id(0), pl.program_id(1)
    rows, cols, _ = x_ref.shape

    @pl.when(i == 0)
    def _():
        sums_ref[...] = jnp.zeros_like(sums_ref)

    @pl.when(slots_ref[o * pl.num_programs(1) + i] >= 0)
    def _():
        xe_ref[1 : rows + 1] = x_ref[...]
        xe_ref[0:1] = top_ref[...]
        xe_ref[rows + 1 : rows + 2] = bottom_ref[...]

        def add(r, total):
            n = total.shape[0]
            sums_ref[0, r : r + n] += total

        stencil(xe_ref, taps_of(weight_ref), rows, cols, 1, add)


def own_sums(slots, image, top, bottom, conv_weight):
    rows, cols, chans = image.shape
    outs, _, taps, size, _ = conv_weight.shape
    own = chans // size
    return pl.pallas_call(
        own_kernel,
        out_shape=jax.ShapeDtypeStruct((outs, rows, cols, size), jnp.float32),
        grid_spec=pltpu.PrefetchScalarGridSpec(
            num_scalar_prefetch=1,
            grid=(outs, own),
            in_specs=[
                pl.BlockSpec((rows, cols, size), lambda o, i, s: (0, 0, i)),
                pl.BlockSpec((1, cols, size), lambda o, i, s: (0, 0, i)),
                pl.BlockSpec((1, cols, size), lambda o, i, s: (0, 0, i)),
                pl.BlockSpec(
                    (1, 1, taps, size, size),
                    lambda o, i, s: (o, jnp.maximum(s[o * own + i], 0), 0, 0, 0),
                ),
            ],
            out_specs=pl.BlockSpec((1, rows, cols, size), lambda o, i, s: (o, 0, 0, 0)),
            scratch_shapes=[pltpu.VMEM((rows + 2, cols, size), jnp.bfloat16)],
        ),
        compiler_params=pltpu.CompilerParams(vmem_limit_bytes=VMEM_BYTES),
        cost_estimate=pl.CostEstimate(
            flops=outs * 2 * taps * rows * cols * size * size, bytes_accessed=30 << 20, transcendentals=0
        ),
        name="own_sums",
    )(slots, image, top, bottom, conv_weight)


def more_kernel(final, slots_ref, one_ref, two_ref, top_ref, bottom_ref, weight_ref, before_ref, *refs):
    if final:
        bias_ref, out_ref, xe_ref, sums_ref = refs
    else:
        sums_ref, xe_ref = refs
    o, d = pl.program_id(0), pl.program_id(1)
    rows, cols, _ = one_ref.shape

    @pl.when(d == 0)
    def _():
        sums_ref[...] = before_ref[...]

    wanted = slots_ref[2 * o + d] >= 0
    for side, x_ref in enumerate((one_ref, two_ref)):

        @pl.when(wanted & (d == side))
        def _(side=side, x_ref=x_ref):
            xe_ref[1 : rows + 1] = x_ref[...]
            xe_ref[0:1] = top_ref[side : side + 1]
            xe_ref[rows + 1 : rows + 2] = bottom_ref[side : side + 1]

    @pl.when(wanted)
    def _():
        def add(r, total):
            n = total.shape[0]
            sums_ref[0, r : r + n] += total

        stencil(xe_ref, taps_of(weight_ref), rows, cols, 1, add)

    if final:

        @pl.when(d == 1)
        def _():
            out_ref[...] = jnp.maximum(sums_ref[0] + bias_ref[...].reshape(1, 1, -1), 0.0).astype(out_ref.dtype)


def more_sums(slots, one, two, top, bottom, conv_weight, sums, bias=None):
    rows, cols, size = one.shape
    outs, _, taps, _, _ = conv_weight.shape
    final = bias is not None
    whole = lambda o, d, s: (0, 0, 0)
    at_out = lambda o, d, s: (o, 0, 0, 0)
    in_specs = [
        pl.BlockSpec((rows, cols, size), whole),
        pl.BlockSpec((rows, cols, size), whole),
        pl.BlockSpec((2, cols, size), whole),
        pl.BlockSpec((2, cols, size), whole),
        pl.BlockSpec((1, 1, taps, size, size), lambda o, d, s: (o, jnp.maximum(s[2 * o + d], 0), 0, 0, 0)),
        pl.BlockSpec((1, rows, cols, size), at_out),
    ]
    args = [slots, one, two, top, bottom, conv_weight, sums]
    scratch = [pltpu.VMEM((rows + 2, cols, size), jnp.bfloat16)]
    if final:
        in_specs.append(pl.BlockSpec((1, size), lambda o, d, s: (0, o)))
        args.append(bias)
        out_shape = jax.ShapeDtypeStruct((rows, cols, outs * size), jnp.bfloat16)
        out_spec = pl.BlockSpec((rows, cols, size), lambda o, d, s: (0, 0, o))
        scratch.append(pltpu.VMEM((1, rows, cols, size), jnp.float32))
        alias = {}
    else:
        out_shape = jax.ShapeDtypeStruct(sums.shape, sums.dtype)
        out_spec = pl.BlockSpec((1, rows, cols, size), at_out)
        alias = {6: 0}
    return pl.pallas_call(
        functools.partial(more_kernel, final),
        out_shape=out_shape,
        grid_spec=pltpu.PrefetchScalarGridSpec(
            num_scalar_prefetch=1, grid=(outs, 2), in_specs=in_specs, out_specs=out_spec, scratch_shapes=scratch
        ),
        input_output_aliases=alias,
        compiler_params=pltpu.CompilerParams(vmem_limit_bytes=VMEM_BYTES),
        cost_estimate=pl.CostEstimate(
            flops=3 * 2 * taps * rows * cols * size * size, bytes_accessed=26 << 20, transcendentals=0
        ),
        name="last_sums" if final else "more_sums",
    )(*args)


def branch_kernel(x_ref, top_ref, bottom_ref, image_ref, weight_ref, out_ref, xe_ref):
    rows, cols, _ = x_ref.shape
    xe_ref[0:2] = top_ref[...]
    xe_ref[2 : rows + 2] = x_ref[...]
    xe_ref[rows + 2 : rows + 4] = bottom_ref[...]

    def add(r, total):
        n = total.shape[0]
        out_ref[r : r + n] = (image_ref[r : r + n].astype(jnp.float32) + total).astype(out_ref.dtype)

    stencil(xe_ref, lambda c: weight_ref[0, c], rows, cols, 2, add)


def branch_out(hidden, top, bottom, image, paired):
    rows, cols, chans = image.shape
    pairs, _, deep, size = paired.shape
    block = lambda n: pl.BlockSpec((n, cols, size), lambda o: (0, 0, o))
    return pl.pallas_call(
        branch_kernel,
        out_shape=jax.ShapeDtypeStruct(image.shape, image.dtype),
        grid=(pairs,),
        in_specs=[
            block(rows),
            block(2),
            block(2),
            block(rows),
            pl.BlockSpec((1, 3, deep, size), lambda o: (o, 0, 0, 0)),
        ],
        out_specs=block(rows),
        scratch_shapes=[pltpu.VMEM((rows + 4, cols, size), jnp.bfloat16)],
        compiler_params=pltpu.CompilerParams(vmem_limit_bytes=VMEM_BYTES),
        cost_estimate=pl.CostEstimate(
            flops=2 * 3 * pairs * deep * size * rows * cols, bytes_accessed=18 << 20, transcendentals=0
        ),
        name="branch_out",
    )(hidden, top, bottom, image, paired)


def pair_weights(group_weight):
    groups, taps, g, _ = group_weight.shape
    w = group_weight.reshape(groups // 2, 2, 3, 3, g, g)
    zero = jnp.zeros_like(w[:, 0])
    upper = jnp.concatenate([w[:, 0], zero], axis=-1)
    lower = jnp.concatenate([zero, w[:, 1]], axis=-1)
    both = jnp.concatenate([upper, lower], axis=-2)
    return both.transpose(0, 2, 1, 3, 4).reshape(groups // 2, 3, 3 * 2 * g, 2 * g)


def along_rows(upper, lower):
    n = lax.axis_size("rows")
    down = [(i, i + 1) for i in range(n - 1)]
    up = [(i + 1, i) for i in range(n - 1)]
    return lax.ppermute(upper, "rows", down), lax.ppermute(lower, "rows", up)


def shards(image, block_links, fan_count, conv_weight, conv_bias, group_weight):
    rows, cols, _ = image.shape
    outs, fan, taps, size, _ = conv_weight.shape
    own = image.shape[2] // size
    blocks = block_links.shape[0]
    chans = lax.axis_size("chan")
    z = lax.axis_index("chan")
    most = most_rounds(chans, own)
    lag = lag_of(own)

    picks, slot_of = make_plan(block_links, fan_count, chans, own, most)
    picks = picks[:, :, 0]
    rounds = jnp.sum(jnp.any(picks >= 0, axis=1).astype(jnp.int32))
    padded = jnp.pad(picks, ((0, 0), (1, 1)), constant_values=-1)
    mirror = chans + chans - 1 - z
    at = lambda r: lax.dynamic_slice_in_dim(padded, r + 1, 1, 1)
    nothing = jnp.full((most, 1), -1, jnp.int32)
    got_left = jnp.where(z > 0, at(z - 1), nothing)
    got_right = jnp.where(z < chans - 1, at(mirror - 1), nothing)
    table = jnp.concatenate([at(z), at(mirror), got_left, got_right], axis=1)
    my_slots = lax.dynamic_slice_in_dim(slot_of, z * outs, outs, 0)[:, :blocks]
    own_slots = lax.dynamic_slice_in_dim(my_slots, z * own, own, 1).reshape(-1)
    arrived = table[:, 2:]
    hit = arrived[:, None, :, None] == jnp.arange(blocks, dtype=jnp.int32)
    more_slots = jnp.max(jnp.where(hit, my_slots[None, :, None, :], -1), axis=-1).reshape(most, outs * 2)
    me = z.reshape(1)
    table = table.reshape(-1)
    paired = pair_weights(group_weight)
    bias = conv_bias.reshape(1, -1)
    right = [(i, i + 1) for i in range(chans - 1)]
    left = [(i + 1, i) for i in range(chans - 1)]

    def run(count):
        from_left, from_right, sums = [], [], None
        hidden = None
        for k in range(count):
            ready = max(k - lag + 1, 0)
            out_right, out_left = choose(
                k, own, size, me, table, image, from_left[:ready], from_right[:ready]
            )
            from_left.append(lax.ppermute(out_right, "chan", right))
            from_right.append(lax.ppermute(out_left, "chan", left))
        top, bottom = along_rows(image[rows - 1 :], image[:1])
        sums = own_sums(own_slots, image, top, bottom, conv_weight)
        for k in range(count):
            one, two = from_left[k], from_right[k]
            top, bottom = along_rows(
                jnp.concatenate([one[rows - 1 :], two[rows - 1 :]], axis=0),
                jnp.concatenate([one[:1], two[:1]], axis=0),
            )
            last = bias if k == count - 1 else None
            sums = more_sums(more_slots[k], one, two, top, bottom, conv_weight, sums, last)
        hidden = sums
        top, bottom = along_rows(hidden[rows - 2 :], hidden[:2])
        return branch_out(hidden, top, bottom, image, paired)

    choices = list(range(blocks // 2, most + 1)) if chans <= 4 else [most]
    if len(choices) == 1:
        return run(choices[0])
    branch = jnp.clip(rounds - choices[0], 0, len(choices) - 1)
    return lax.switch(branch, [functools.partial(run, n) for n in choices])


def solution(mesh):
    in_specs = (
        P(("groups", "rows"), None, "chan"),
        P(),
        P(),
        P("chan", None, None, None, None),
        P("chan"),
        P("chan", None, None, None),
    )
    out_specs = P(("groups", "rows"), None, "chan")
    return jax.shard_map(shards, mesh=mesh, in_specs=in_specs, out_specs=out_specs, check_vma=False)
```

```python
import functools

import jax
import jax.numpy as jnp
from jax import lax
from jax.experimental import pallas as pl
from jax.experimental.pallas import tpu as pltpu
from jax.sharding import PartitionSpec as P

LANES = 128
VMEM_BYTES = 48 << 20


def lag_of(own):
    return 2 if own >= 2 else 1


def most_rounds(chans, own):
    lag = lag_of(own)
    return max(hop * lag + (chans - 1 - hop) * own for hop in range(chans - 1))


def plan_kernel(chans, own, rounds, links_ref, fans_ref, pick_ref, slot_ref):
    blocks, fan = links_ref.shape
    lag = lag_of(own)
    lane = lax.broadcasted_iota(jnp.int32, (blocks, LANES), 1)
    links = links_ref[...]
    fans = fans_ref[...]
    slot = jnp.full((blocks, LANES), -1, jnp.int32)
    for s in range(fan):
        slot = jnp.where((links[:, s : s + 1] == lane) & (fans > s), s, slot)
    slot_ref[...] = slot
    used = jnp.where(slot >= 0, 1.0, 0.0)
    far = jnp.full((1, LANES), -1.0, jnp.float32)
    near = jnp.full((1, LANES), float(chans), jnp.float32)
    for z in range(chans):
        up = jnp.max(used[z * own : (z + 1) * own], axis=0, keepdims=True)
        far = jnp.where(up > 0, float(z), far)
        w = chans - 1 - z
        down = jnp.max(used[w * own : (w + 1) * own], axis=0, keepdims=True)
        near = jnp.where(down > 0, float(w), near)
    shape = (2 * chans, LANES)
    row = lax.broadcasted_iota(jnp.int32, shape, 0)
    block = lax.broadcasted_iota(jnp.int32, shape, 1)
    mirrored = row >= chans
    here = jnp.where(mirrored, row - chans, row).astype(jnp.float32)
    home = jnp.zeros(shape, jnp.float32)
    for z in range(1, chans):
        home = home + jnp.where(block >= z * own, 1.0, 0.0)
    home = jnp.where(mirrored, chans - 1.0 - home, home)
    reach = jnp.where(mirrored, chans - 1.0 - near, far)
    blockf = block.astype(jnp.float32)
    left = jnp.where((reach > here) & (home <= here) & (block < blocks), 1.0, 0.0)
    held = jnp.where(home == here, 1.0, 0.0)
    rank = reach * 4096.0 + home * 128.0 + blockf
    sent = []
    for k in range(rounds):
        if k >= lag:
            held = jnp.maximum(held, pltpu.roll(sent[k - lag], 1, 0))
        score = jnp.where((left > 0) & (held > 0), rank, -1.0)
        best = jnp.max(score, axis=1, keepdims=True)
        chosen = jnp.where((score == best) & (best >= 0), 1.0, 0.0)
        sent.append(chosen)
        left = left - chosen
        which = jnp.max(jnp.where(chosen > 0, blockf, -1.0), axis=1, keepdims=True)
        pick_ref[k] = jnp.broadcast_to(which, shape).astype(jnp.int32)


def make_plan(block_links, fan_count, chans, own, rounds):
    blocks = block_links.shape[0]
    return pl.pallas_call(
        functools.partial(plan_kernel, chans, own, rounds),
        out_shape=(
            jax.ShapeDtypeStruct((rounds, 2 * chans, LANES), jnp.int32),
            jax.ShapeDtypeStruct((blocks, LANES), jnp.int32),
        ),
        name="plan",
    )(block_links, fan_count.reshape(blocks, 1))


def choose_kernel(k, own, size, held, me_ref, table_ref, image_ref, *refs):
    from_left, from_right = refs[:held], refs[held : 2 * held]
    right_ref, left_ref, sems = refs[-3:]
    base = me_ref[0] * own
    for d, (out_ref, got) in enumerate(((right_ref, from_left), (left_ref, from_right))):
        block = table_ref[4 * k + d]
        mine = (block >= base) & (block < base + own)

        @pl.when(mine)
        def _(d=d, out_ref=out_ref, block=block):
            start = pl.multiple_of((block - base) * size, size)
            pltpu.make_async_copy(image_ref.at[:, :, pl.ds(start, size)], out_ref, sems.at[d]).start()

        for j in range(held):
            same = (block >= 0) & jnp.logical_not(mine) & (table_ref[4 * j + 2 + d] == block)

            @pl.when(same)
            def _(d=d, out_ref=out_ref, ref=got[j]):
                pltpu.make_async_copy(ref, out_ref, sems.at[d]).start()

    for d, out_ref in enumerate((right_ref, left_ref)):

        @pl.when(table_ref[4 * k + d] >= 0)
        def _(d=d, out_ref=out_ref):
            pltpu.make_async_copy(image_ref.at[:, :, pl.ds(0, size)], out_ref, sems.at[d]).wait()


def choose(k, own, size, me, table, image, from_left, from_right, after):
    rows, cols, _ = image.shape
    shape = jax.ShapeDtypeStruct((rows, cols, size), image.dtype)
    anywhere = pl.BlockSpec(memory_space=pl.ANY)
    scalars = pl.BlockSpec(memory_space=pltpu.SMEM)
    return pl.pallas_call(
        functools.partial(choose_kernel, k, own, size, len(from_left)),
        out_shape=(shape, shape),
        in_specs=[scalars, scalars] + [anywhere] * (1 + len(from_left) + len(from_right) + len(after)),
        out_specs=(pl.BlockSpec(memory_space=pltpu.VMEM),) * 2,
        scratch_shapes=[pltpu.SemaphoreType.DMA((2,))],
        compiler_params=pltpu.CompilerParams(vmem_limit_bytes=VMEM_BYTES),
        cost_estimate=pl.CostEstimate(flops=0, bytes_accessed=4 * rows * cols * size * 2, transcendentals=0),
        name=f"choose_{k}",
    )(me, table, image, *from_left, *from_right, *after)


def shifted(y, step, col):
    cols = y.shape[1]
    moved = pltpu.roll(y, step % cols, 1)
    return jnp.where((col >= step) & (col < cols + step), moved, 0.0)


def stencil(xe_ref, weight_of, rows, cols, gap, add):
    step = 4
    width = xe_ref.shape[2]
    col = lax.broadcasted_iota(jnp.int32, (step, cols, 1), 1)

    def few(i, carry):
        r = i * step
        wide = jnp.concatenate(
            [xe_ref[pl.ds(r + a * gap, step)].reshape(step * cols, width) for a in range(3)], axis=1
        )
        total = None
        for c in range(3):
            y = jnp.dot(wide, weight_of(c), preferred_element_type=jnp.float32)
            y = y.reshape(step, cols, y.shape[-1])
            if c != 1:
                y = shifted(y, (1 - c) * gap, col)
            total = y if total is None else total + y
        add(r, step, total)
        return carry

    lax.fori_loop(0, rows // step, few, 0)


def source_in(code):
    return (code >> 2) & 63


def output_in(code):
    return (code >> 8) & 255


def kernel_in(code):
    return (code >> 16) & 255, code >> 24


def compact_steps(slots, sources):
    count = slots.shape[1]
    valid = slots >= 0
    index = jnp.arange(count, dtype=jnp.int32)
    place = jnp.sum(jnp.where(valid[:, None, :] & (index[None, :] < index[:, None])[None], 1, 0), axis=2)
    total = jnp.sum(valid.astype(jnp.int32), axis=1, keepdims=True)
    want = jnp.minimum(index[None, :], jnp.maximum(total - 1, 0))
    pick = valid[:, None, :] & (place[:, None, :] == want[:, :, None])
    take = lambda v: jnp.sum(jnp.where(pick, v, 0), axis=2)
    entry = take(index[None, None, :])
    out = entry // sources
    slot = take(slots[:, None, :])
    active = (index[None, :] < total).astype(jnp.int32)
    before = jnp.concatenate([jnp.full_like(out[:, :1], -1), out[:, :-1]], axis=1)
    first = (out != before).astype(jnp.int32)
    return active | (first << 1) | ((entry % sources) << 2) | (out << 8) | (out << 16) | (slot << 24)


def every_step(slots, sources, keep=False):
    count = slots.shape[1]
    valid = slots >= 0
    index = jnp.arange(count, dtype=jnp.int32)
    up_to = (index[None, :] <= index[:, None])[None]
    latest = jnp.max(jnp.where(valid[:, None, :] & up_to, index[None, None, :], -1), axis=2)
    soonest = jnp.min(jnp.where(valid, index[None, :], count - 1), axis=1, keepdims=True)
    entry = jnp.where(latest >= 0, latest, soonest)
    pick = entry[:, :, None] == index[None, None, :]
    slot = jnp.maximum(jnp.sum(jnp.where(pick, slots[:, None, :], 0), axis=2), 0)
    first = (index % sources == 0).astype(jnp.int32)
    source = entry % sources if keep else (index % sources)[None]
    fixed = (first << 1) | ((index // sources) << 8)
    return valid.astype(jnp.int32) | fixed[None] | (source << 2) | ((entry // sources) << 16) | (slot << 24)


def fill(xe_ref, x_ref, top, bottom):
    rows = x_ref.shape[0]
    xe_ref[1 : rows + 1] = x_ref[...]
    xe_ref[0:1] = top
    xe_ref[rows + 1 : rows + 2] = bottom


def add_block(xe_ref, weight_ref, sums_ref):
    _, rows, cols, _ = sums_ref.shape

    def weight_of(c):
        return jnp.concatenate([weight_ref[0, 0, 3 * a + c] for a in range(3)], axis=0)

    def add(r, n, total):
        sums_ref[0, pl.ds(r, n)] += total

    stencil(xe_ref, weight_of, rows, cols, 1, add)


LIGHT = pl.CostEstimate(flops=0, bytes_accessed=1 << 20, transcendentals=0)


def own_kernel(codes_ref, x_ref, top_ref, bottom_ref, weight_ref, _, sums_ref, xe_ref):
    code = codes_ref[pl.program_id(0)]

    @pl.when((code & 2) > 0)
    def _():
        sums_ref[...] = jnp.zeros_like(sums_ref)

    @pl.when((code & 1) > 0)
    def _():
        fill(xe_ref, x_ref, top_ref[...], bottom_ref[...])
        add_block(xe_ref, weight_ref, sums_ref)


def own_sums(codes, image, top, bottom, conv_weight, after):
    rows, cols, _ = image.shape
    outs, _, taps, size, _ = conv_weight.shape
    source = lambda i, s: (0, 0, source_in(s[i]))

    def weights(i, s):
        out, slot = kernel_in(s[i])
        return out, slot, 0, 0, 0

    return pl.pallas_call(
        own_kernel,
        out_shape=jax.ShapeDtypeStruct((outs, rows, cols, size), jnp.float32),
        grid_spec=pltpu.PrefetchScalarGridSpec(
            num_scalar_prefetch=1,
            grid=(codes.shape[0],),
            in_specs=[
                pl.BlockSpec((rows, cols, size), source),
                pl.BlockSpec((1, cols, size), source),
                pl.BlockSpec((1, cols, size), source),
                pl.BlockSpec((1, 1, taps, size, size), weights),
                pl.BlockSpec(memory_space=pl.ANY),
            ],
            out_specs=pl.BlockSpec((1, rows, cols, size), lambda i, s: (output_in(s[i]), 0, 0, 0)),
            scratch_shapes=[pltpu.VMEM((rows + 2, cols, size), jnp.bfloat16)],
        ),
        compiler_params=pltpu.CompilerParams(vmem_limit_bytes=VMEM_BYTES),
        cost_estimate=LIGHT,
        name="own_sums",
    )(codes, image, top, bottom, conv_weight, after)


def more_kernel(final, count, codes_ref, *refs):
    xs, refs = refs[:count], refs[count:]
    top_ref, bottom_ref, weight_ref, before_ref = refs[:4]
    if final:
        bias_ref, out_ref, head_ref, tail_ref, xe_ref, sums_ref = refs[4:]
    else:
        _, sums_ref, xe_ref = refs[4:]
    code = codes_ref[pl.program_id(0)]

    @pl.when((code & 2) > 0)
    def _():
        sums_ref[...] = before_ref[...]

    @pl.when((code & 1) > 0)
    def _():
        for side, x_ref in enumerate(xs):

            @pl.when(source_in(code) == side)
            def _(side=side, x_ref=x_ref):
                fill(xe_ref, x_ref, top_ref[side : side + 1], bottom_ref[side : side + 1])

        add_block(xe_ref, weight_ref, sums_ref)

    if final:

        @pl.when(source_in(code) == count - 1)
        def _():
            out = jnp.maximum(sums_ref[0] + bias_ref[...].reshape(1, 1, -1), 0.0).astype(out_ref.dtype)
            rows = out.shape[0]
            out_ref[...] = out
            head_ref[...] = out[:2]
            tail_ref[...] = out[rows - 2 :]


def more_sums(codes, xs, top, bottom, conv_weight, sums, after=None, bias=None):
    rows, cols, size = xs[0].shape
    outs, _, taps, _, _ = conv_weight.shape
    final = bias is not None
    whole = lambda i, s: (0, 0, 0)
    at_out = lambda i, s: (output_in(s[i]), 0, 0, 0)
    in_channels = lambda n: pl.BlockSpec((n, cols, size), lambda i, s: (0, 0, output_in(s[i])))

    def weights(i, s):
        out, slot = kernel_in(s[i])
        return out, slot, 0, 0, 0

    in_specs = [pl.BlockSpec((rows, cols, size), whole)] * len(xs) + [
        pl.BlockSpec((len(xs), cols, size), whole),
        pl.BlockSpec((len(xs), cols, size), whole),
        pl.BlockSpec((1, 1, taps, size, size), weights),
        pl.BlockSpec((1, rows, cols, size), at_out),
    ]
    args = [codes, *xs, top, bottom, conv_weight, sums]
    scratch = [pltpu.VMEM((rows + 2, cols, size), jnp.bfloat16)]
    if final:
        in_specs.append(pl.BlockSpec((1, size), lambda i, s: (0, output_in(s[i]))))
        args.append(bias)
        heights = (rows, 2, 2)
        out_shape = tuple(jax.ShapeDtypeStruct((n, cols, outs * size), jnp.bfloat16) for n in heights)
        out_specs = tuple(in_channels(n) for n in heights)
        scratch.append(pltpu.VMEM((1, rows, cols, size), jnp.float32))
        alias = {}
    else:
        in_specs.append(pl.BlockSpec(memory_space=pl.ANY))
        args.append(after)
        out_shape = jax.ShapeDtypeStruct(sums.shape, sums.dtype)
        out_specs = pl.BlockSpec((1, rows, cols, size), at_out)
        alias = {4 + len(xs): 0}
    return pl.pallas_call(
        functools.partial(more_kernel, final, len(xs)),
        out_shape=out_shape,
        grid_spec=pltpu.PrefetchScalarGridSpec(
            num_scalar_prefetch=1,
            grid=(codes.shape[0],),
            in_specs=in_specs,
            out_specs=out_specs,
            scratch_shapes=scratch,
        ),
        input_output_aliases=alias,
        compiler_params=pltpu.CompilerParams(vmem_limit_bytes=VMEM_BYTES),
        cost_estimate=LIGHT,
        name="last_sums" if final else "more_sums",
    )(*args)


def branch_kernel(x_ref, top_ref, bottom_ref, image_ref, weight_ref, out_ref, xe_ref):
    rows, cols, _ = x_ref.shape
    xe_ref[0:2] = top_ref[...]
    xe_ref[2 : rows + 2] = x_ref[...]
    xe_ref[rows + 2 : rows + 4] = bottom_ref[...]

    def weight_of(c):
        return jnp.concatenate([weight_ref[0, 3 * a + c] for a in range(3)], axis=0)

    def add(r, n, total):
        at = pl.ds(r, n)
        out_ref[at] = (image_ref[at].astype(jnp.float32) + total).astype(out_ref.dtype)

    stencil(xe_ref, weight_of, rows, cols, 2, add)


def branch_out(hidden, top, bottom, image, paired):
    rows, cols, chans = image.shape
    pairs, taps, size, _ = paired.shape
    block = lambda n: pl.BlockSpec((n, cols, size), lambda o: (0, 0, o))
    return pl.pallas_call(
        branch_kernel,
        out_shape=jax.ShapeDtypeStruct(image.shape, image.dtype),
        grid=(pairs,),
        in_specs=[
            block(rows),
            block(2),
            block(2),
            block(rows),
            pl.BlockSpec((1, taps, size, size), lambda o: (o, 0, 0, 0)),
        ],
        out_specs=block(rows),
        scratch_shapes=[pltpu.VMEM((rows + 4, cols, size), jnp.bfloat16)],
        compiler_params=pltpu.CompilerParams(vmem_limit_bytes=VMEM_BYTES),
        cost_estimate=LIGHT,
        name="branch_out",
    )(hidden, top, bottom, image, paired)


def pair_weights(group_weight):
    groups, taps, g, _ = group_weight.shape
    w = group_weight.reshape(groups // 2, 2, taps, g, g)
    upper = jnp.pad(w[:, 0], ((0, 0), (0, 0), (0, g), (0, g)))
    lower = jnp.pad(w[:, 1], ((0, 0), (0, 0), (g, 0), (g, 0)))
    return upper + lower


def along_rows(upper, lower):
    n = lax.axis_size("rows")
    down = [(i, i + 1) for i in range(n - 1)]
    up = [(i + 1, i) for i in range(n - 1)]
    return lax.ppermute(upper, "rows", down), lax.ppermute(lower, "rows", up)


def shards(image, block_links, fan_count, conv_weight, conv_bias, group_weight):
    rows, cols, _ = image.shape
    outs, fan, taps, size, _ = conv_weight.shape
    own = image.shape[2] // size
    blocks = block_links.shape[0]
    chans = lax.axis_size("chan")
    z = lax.axis_index("chan")
    most = most_rounds(chans, own)
    lag = lag_of(own)

    picks, slot_of = make_plan(block_links, fan_count, chans, own, most)
    picks = picks[:, :, 0]
    rounds = jnp.sum(jnp.any(picks >= 0, axis=1).astype(jnp.int32))
    padded = jnp.pad(picks, ((0, 0), (1, 1)), constant_values=-1)
    mirror = chans + chans - 1 - z
    at = lambda r: lax.dynamic_slice_in_dim(padded, r + 1, 1, 1)
    nothing = jnp.full((most, 1), -1, jnp.int32)
    got_left = jnp.where(z > 0, at(z - 1), nothing)
    got_right = jnp.where(z < chans - 1, at(mirror - 1), nothing)
    table = jnp.concatenate([at(z), at(mirror), got_left, got_right], axis=1)
    my_slots = lax.dynamic_slice_in_dim(slot_of, z * outs, outs, 0)[:, :blocks]
    own_slots = lax.dynamic_slice_in_dim(my_slots, z * own, own, 1).reshape(1, -1)
    arrived = table[:, 2:]
    hit = arrived[:, None, :, None] == jnp.arange(blocks, dtype=jnp.int32)
    single = jnp.max(jnp.where(hit, my_slots[None, :, None, :], -1), axis=-1)
    even = most + most % 2
    double = jnp.pad(single, ((0, even - most), (0, 0), (0, 0)), constant_values=-1)
    double = double.reshape(even // 2, 2, outs, 2).transpose(0, 2, 1, 3).reshape(even // 2, outs * 4)
    single = single.reshape(most, outs * 2)
    own_steps = every_step(own_slots, own, keep=True)[0]
    double_steps = compact_steps(double, 4)
    single_steps = compact_steps(single, 2)
    last_steps = every_step(single, 2)
    me = z.reshape(1)
    table = table.reshape(-1)
    paired = pair_weights(group_weight)
    bias = conv_bias.reshape(1, -1)
    right = [(i, i + 1) for i in range(chans - 1)]
    left = [(i + 1, i) for i in range(chans - 1)]

    def run(count):
        from_left, from_right = [], []
        own_rims = along_rows(image[rows - 1 :], image[:1])
        sums = out_right = None
        done = 0

        def rims(xs):
            return along_rows(
                jnp.concatenate([x[rows - 1 :] for x in xs], axis=0), jnp.concatenate([x[:1] for x in xs], axis=0)
            )

        def add_rounds(n, sums, out_right):
            steps = double_steps[done // 2] if n == 2 else single_steps[done]
            xs = [x for k in range(done, done + n) for x in (from_left[k], from_right[k])]
            return more_sums(steps, xs, *rims(xs), conv_weight, sums, out_right)

        for k in range(count + 1):
            if k < count:
                ready = max(k - lag + 1, 0)
                out_right, out_left = choose(
                    k, own, size, me, table, image, from_left[:ready], from_right[:ready], [] if sums is None else [sums]
                )
                from_left.append(lax.ppermute(out_right, "chan", right))
                from_right.append(lax.ppermute(out_left, "chan", left))
            if k == 1:
                sums = own_sums(own_steps, image, *own_rims, conv_weight, out_right)
            while done + 2 <= min(k - 1, count - 1):
                sums = add_rounds(2, sums, out_right)
                done += 2
        while done < count - 1:
            sums = add_rounds(1, sums, out_right)
            done += 1
        xs = [from_left[-1], from_right[-1]]
        hidden, head, tail = more_sums(last_steps[count - 1], xs, *rims(xs), conv_weight, sums, bias=bias)
        return branch_out(hidden, *along_rows(tail, head), image, paired)

    choices = list(range(blocks // 2, most + 1)) if chans <= 4 else [most]
    if len(choices) == 1:
        return run(choices[0])
    branch = jnp.clip(rounds - choices[0], 0, len(choices) - 1)
    return lax.switch(branch, [functools.partial(run, n) for n in choices])


def solution(mesh):
    in_specs = (
        P(("groups", "rows"), None, "chan"),
        P(),
        P(),
        P("chan", None, None, None, None),
        P("chan"),
        P("chan", None, None, None),
    )
    out_specs = P(("groups", "rows"), None, "chan")
    return jax.shard_map(shards, mesh=mesh, in_specs=in_specs, out_specs=out_specs, check_vma=False)
```

```python
import functools

import jax
import jax.numpy as jnp
from jax import lax
from jax.experimental import pallas as pl
from jax.experimental.pallas import tpu as pltpu
from jax.sharding import PartitionSpec as P

LANES = 128
VMEM_BYTES = 48 << 20


def lag_of(own):
    return 2 if own >= 2 else 1


def most_rounds(chans, own):
    lag = lag_of(own)
    return max(hop * lag + (chans - 1 - hop) * own for hop in range(chans - 1))


def plan_kernel(chans, own, rounds, links_ref, fans_ref, pick_ref, slot_ref):
    blocks, fan = links_ref.shape
    lag = lag_of(own)
    lane = lax.broadcasted_iota(jnp.int32, (blocks, LANES), 1)
    links = links_ref[...]
    fans = fans_ref[...]
    slot = jnp.full((blocks, LANES), -1, jnp.int32)
    for s in range(fan):
        slot = jnp.where((links[:, s : s + 1] == lane) & (fans > s), s, slot)
    slot_ref[...] = slot
    used = jnp.where(slot >= 0, 1.0, 0.0)
    far = jnp.full((1, LANES), -1.0, jnp.float32)
    near = jnp.full((1, LANES), float(chans), jnp.float32)
    for z in range(chans):
        up = jnp.max(used[z * own : (z + 1) * own], axis=0, keepdims=True)
        far = jnp.where(up > 0, float(z), far)
        w = chans - 1 - z
        down = jnp.max(used[w * own : (w + 1) * own], axis=0, keepdims=True)
        near = jnp.where(down > 0, float(w), near)
    shape = (2 * chans, LANES)
    row = lax.broadcasted_iota(jnp.int32, shape, 0)
    block = lax.broadcasted_iota(jnp.int32, shape, 1)
    mirrored = row >= chans
    here = jnp.where(mirrored, row - chans, row).astype(jnp.float32)
    home = jnp.zeros(shape, jnp.float32)
    for z in range(1, chans):
        home = home + jnp.where(block >= z * own, 1.0, 0.0)
    home = jnp.where(mirrored, chans - 1.0 - home, home)
    reach = jnp.where(mirrored, chans - 1.0 - near, far)
    blockf = block.astype(jnp.float32)
    left = jnp.where((reach > here) & (home <= here) & (block < blocks), 1.0, 0.0)
    held = jnp.where(home == here, 1.0, 0.0)
    rank = reach * 4096.0 + home * 128.0 + blockf
    sent = []
    for k in range(rounds):
        if k >= lag:
            held = jnp.maximum(held, pltpu.roll(sent[k - lag], 1, 0))
        score = jnp.where((left > 0) & (held > 0), rank, -1.0)
        best = jnp.max(score, axis=1, keepdims=True)
        chosen = jnp.where((score == best) & (best >= 0), 1.0, 0.0)
        sent.append(chosen)
        left = left - chosen
        which = jnp.max(jnp.where(chosen > 0, blockf, -1.0), axis=1, keepdims=True)
        pick_ref[k] = jnp.broadcast_to(which, shape).astype(jnp.int32)


def make_plan(block_links, fan_count, chans, own, rounds):
    blocks = block_links.shape[0]
    return pl.pallas_call(
        functools.partial(plan_kernel, chans, own, rounds),
        out_shape=(
            jax.ShapeDtypeStruct((rounds, 2 * chans, LANES), jnp.int32),
            jax.ShapeDtypeStruct((blocks, LANES), jnp.int32),
        ),
        name="plan",
    )(block_links, fan_count.reshape(blocks, 1))


def quarters(rows):
    step = rows // 4
    return [pl.ds(i * step, step) for i in range(4)]


def choose_kernel(k, own, size, held, me_ref, table_ref, image_ref, *refs):
    from_left, from_right = refs[:held], refs[held : 2 * held]
    right_ref, left_ref, sems = refs[-3:]
    base = me_ref[0] * own
    for d, (out_ref, got) in enumerate(((right_ref, from_left), (left_ref, from_right))):
        block = table_ref[4 * k + d]
        mine = (block >= base) & (block < base + own)

        @pl.when(mine)
        def _(d=d, out_ref=out_ref, block=block):
            start = pl.multiple_of((block - base) * size, size)
            for at in quarters(out_ref.shape[0]):
                pltpu.make_async_copy(image_ref.at[at, :, pl.ds(start, size)], out_ref.at[at], sems.at[d]).start()

        for j in range(held):
            same = (block >= 0) & jnp.logical_not(mine) & (table_ref[4 * j + 2 + d] == block)

            @pl.when(same)
            def _(d=d, out_ref=out_ref, ref=got[j]):
                for at in quarters(out_ref.shape[0]):
                    pltpu.make_async_copy(ref.at[at], out_ref.at[at], sems.at[d]).start()

    for d, out_ref in enumerate((right_ref, left_ref)):

        @pl.when(table_ref[4 * k + d] >= 0)
        def _(d=d, out_ref=out_ref):
            pltpu.make_async_copy(image_ref.at[:, :, pl.ds(0, size)], out_ref, sems.at[d]).wait()


def choose(k, own, size, me, table, image, from_left, from_right, after):
    rows, cols, _ = image.shape
    shape = jax.ShapeDtypeStruct((rows, cols, size), image.dtype)
    anywhere = pl.BlockSpec(memory_space=pl.ANY)
    scalars = pl.BlockSpec(memory_space=pltpu.SMEM)
    return pl.pallas_call(
        functools.partial(choose_kernel, k, own, size, len(from_left)),
        out_shape=(shape, shape),
        in_specs=[scalars, scalars] + [anywhere] * (1 + len(from_left) + len(from_right) + len(after)),
        out_specs=(pl.BlockSpec(memory_space=pltpu.VMEM),) * 2,
        scratch_shapes=[pltpu.SemaphoreType.DMA((2,))],
        compiler_params=pltpu.CompilerParams(vmem_limit_bytes=VMEM_BYTES),
        cost_estimate=pl.CostEstimate(flops=0, bytes_accessed=4 * rows * cols * size * 2, transcendentals=0),
        name=f"choose_{k}",
    )(me, table, image, *from_left, *from_right, *after)


def shifted(y, step, col):
    cols = y.shape[1]
    moved = pltpu.roll(y, step % cols, 1)
    return jnp.where((col >= step) & (col < cols + step), moved, 0.0)


def stencil(xe_ref, weight_of, rows, cols, gap, add):
    step = 4
    width = xe_ref.shape[2]
    col = lax.broadcasted_iota(jnp.int32, (step, cols, 1), 1)

    def few(i, carry):
        r = i * step
        wide = jnp.concatenate(
            [xe_ref[pl.ds(r + a * gap, step)].reshape(step * cols, width) for a in range(3)], axis=1
        )
        total = None
        for c in range(3):
            y = jnp.dot(wide, weight_of(c), preferred_element_type=jnp.float32)
            y = y.reshape(step, cols, y.shape[-1])
            if c != 1:
                y = shifted(y, (1 - c) * gap, col)
            total = y if total is None else total + y
        add(r, step, total)
        return carry

    lax.fori_loop(0, rows // step, few, 0, unroll=True)


def source_in(code):
    return (code >> 2) & 63


def output_in(code):
    return (code >> 8) & 255


def kernel_in(code):
    return (code >> 16) & 255, code >> 24


def compact_steps(slots, sources, part=0, parts=1):
    count = slots.shape[1]
    valid = slots >= 0
    index = jnp.arange(count, dtype=jnp.int32)
    place = jnp.sum(jnp.where(valid[:, None, :] & (index[None, :] < index[:, None])[None], 1, 0), axis=2)
    total = jnp.sum(valid.astype(jnp.int32), axis=1, keepdims=True)
    skipped = jnp.zeros_like(total)
    step = index
    if parts == 2:
        half = (total + 1) >> 1
        skipped, total = (half, total - half) if part else (skipped, half)
        step = index[: (count + 1) // 2]
    want = skipped + jnp.minimum(step[None, :], jnp.maximum(total - 1, 0))
    pick = valid[:, None, :] & (place[:, None, :] == want[:, :, None])
    take = lambda v: jnp.sum(jnp.where(pick, v, 0), axis=2)
    entry = take(index[None, None, :])
    out = entry // sources
    slot = take(slots[:, None, :])
    active = (step[None, :] < total).astype(jnp.int32)
    before = jnp.concatenate([jnp.full_like(out[:, :1], -1), out[:, :-1]], axis=1)
    first = (out != before).astype(jnp.int32)
    return active | (first << 1) | ((entry % sources) << 2) | (out << 8) | (out << 16) | (slot << 24)


def every_step(slots, sources, keep=False):
    count = slots.shape[1]
    valid = slots >= 0
    index = jnp.arange(count, dtype=jnp.int32)
    up_to = (index[None, :] <= index[:, None])[None]
    latest = jnp.max(jnp.where(valid[:, None, :] & up_to, index[None, None, :], -1), axis=2)
    soonest = jnp.min(jnp.where(valid, index[None, :], count - 1), axis=1, keepdims=True)
    entry = jnp.where(latest >= 0, latest, soonest)
    pick = entry[:, :, None] == index[None, None, :]
    slot = jnp.maximum(jnp.sum(jnp.where(pick, slots[:, None, :], 0), axis=2), 0)
    first = (index % sources == 0).astype(jnp.int32)
    source = entry % sources if keep else (index % sources)[None]
    fixed = (first << 1) | ((index // sources) << 8)
    return valid.astype(jnp.int32) | fixed[None] | (source << 2) | ((entry // sources) << 16) | (slot << 24)


def fill(xe_ref, x_ref, top, bottom):
    rows = x_ref.shape[0]
    xe_ref[1 : rows + 1] = x_ref[...]
    xe_ref[0:1] = top
    xe_ref[rows + 1 : rows + 2] = bottom


def add_block(xe_ref, weight_ref, sums_ref):
    _, rows, cols, _ = sums_ref.shape

    def weight_of(c):
        return jnp.concatenate([weight_ref[0, 0, 3 * a + c] for a in range(3)], axis=0)

    def add(r, n, total):
        sums_ref[0, pl.ds(r, n)] += total

    stencil(xe_ref, weight_of, rows, cols, 1, add)


def rims_kernel(count, *refs):
    xs, (last_ref, first_ref, sems) = refs[:count], refs[-3:]
    copies = []
    for i, x_ref in enumerate(xs):
        rows = x_ref.shape[0]
        for d, (row, out_ref) in enumerate(((rows - 1, last_ref), (0, first_ref))):
            copies.append(
                pltpu.make_async_copy(x_ref.at[pl.ds(row, 1)], out_ref.at[pl.ds(i, 1)], sems.at[d, i])
            )
    for copy in copies:
        copy.start()
    for copy in copies:
        copy.wait()


def rims_of(xs, after):
    _, cols, size = xs[0].shape
    shape = jax.ShapeDtypeStruct((len(xs), cols, size), xs[0].dtype)
    return pl.pallas_call(
        functools.partial(rims_kernel, len(xs)),
        out_shape=(shape, shape),
        in_specs=[pl.BlockSpec(memory_space=pl.ANY)] * (len(xs) + 1),
        out_specs=(pl.BlockSpec(memory_space=pltpu.VMEM),) * 2,
        scratch_shapes=[pltpu.SemaphoreType.DMA((2, len(xs)))],
        compiler_params=pltpu.CompilerParams(vmem_limit_bytes=VMEM_BYTES),
        cost_estimate=LIGHT,
        name="rims",
    )(*xs, after)


LIGHT = pl.CostEstimate(flops=0, bytes_accessed=1 << 20, transcendentals=0)


def own_kernel(codes_ref, x_ref, top_ref, bottom_ref, weight_ref, *refs):
    sums_ref, xe_ref = refs[-2:]
    code = codes_ref[pl.program_id(0)]

    @pl.when((code & 2) > 0)
    def _():
        sums_ref[...] = jnp.zeros_like(sums_ref)

    @pl.when((code & 1) > 0)
    def _():
        fill(xe_ref, x_ref, top_ref[...], bottom_ref[...])
        add_block(xe_ref, weight_ref, sums_ref)


def own_sums(codes, image, top, bottom, conv_weight, after, before=None):
    rows, cols, _ = image.shape
    outs, _, taps, size, _ = conv_weight.shape
    source = lambda i, s: (0, 0, source_in(s[i]))
    extra = [after] if before is None else [after, before]

    def weights(i, s):
        out, slot = kernel_in(s[i])
        return out, slot, 0, 0, 0

    return pl.pallas_call(
        own_kernel,
        out_shape=jax.ShapeDtypeStruct((outs, rows, cols, size), jnp.float32),
        grid_spec=pltpu.PrefetchScalarGridSpec(
            num_scalar_prefetch=1,
            grid=(codes.shape[0],),
            in_specs=[
                pl.BlockSpec((rows, cols, size), source),
                pl.BlockSpec((1, cols, size), source),
                pl.BlockSpec((1, cols, size), source),
                pl.BlockSpec((1, 1, taps, size, size), weights),
            ]
            + [pl.BlockSpec(memory_space=pl.ANY)] * len(extra),
            out_specs=pl.BlockSpec((1, rows, cols, size), lambda i, s: (output_in(s[i]), 0, 0, 0)),
            scratch_shapes=[pltpu.VMEM((rows + 2, cols, size), jnp.bfloat16)],
        ),
        compiler_params=pltpu.CompilerParams(vmem_limit_bytes=VMEM_BYTES),
        input_output_aliases={} if before is None else {6: 0},
        cost_estimate=LIGHT,
        name="own_sums",
    )(codes, image, top, bottom, conv_weight, *extra)


def more_kernel(final, count, codes_ref, *refs):
    xs, refs = refs[:count], refs[count:]
    top_ref, bottom_ref, weight_ref, before_ref = refs[:4]
    if final:
        bias_ref, out_ref, head_ref, tail_ref, xe_ref, sems, sums_ref = refs[4:]
    else:
        _, sums_ref, xe_ref, sems = refs[4:]
    step, steps = pl.program_id(0), codes_ref.shape[0]
    code = codes_ref[step]
    now = lax.rem(step, 2)
    rows = xs[0].shape[0]

    def fetch(code, slot):
        for side, x_ref in enumerate(xs):

            @pl.when(((code & 1) > 0) & (source_in(code) == side))
            def _(x_ref=x_ref):
                for at in quarters(rows):
                    into = xe_ref.at[slot, pl.ds(at.start + 1, at.size)]
                    pltpu.make_async_copy(x_ref.at[at], into, sems.at[slot]).start()

    @pl.when(step == 0)
    def _():
        fetch(code, 0)

    @pl.when(step + 1 < steps)
    def _():
        fetch(codes_ref[jnp.minimum(step + 1, steps - 1)], 1 - now)

    @pl.when((code & 2) > 0)
    def _():
        sums_ref[...] = before_ref[...]

    @pl.when((code & 1) > 0)
    def _():
        side = source_in(code)
        xe_ref[now, 0] = top_ref[side]
        xe_ref[now, rows + 1] = bottom_ref[side]
        pltpu.make_async_copy(xs[0], xe_ref.at[now, pl.ds(1, rows)], sems.at[now]).wait()
        add_block(xe_ref.at[now], weight_ref, sums_ref)

    if final:

        @pl.when(source_in(code) == count - 1)
        def _():
            out = jnp.maximum(sums_ref[0] + bias_ref[...].reshape(1, 1, -1), 0.0).astype(out_ref.dtype)
            out_ref[...] = out
            head_ref[...] = out[:2]
            tail_ref[...] = out[rows - 2 :]


def more_sums(codes, xs, top, bottom, conv_weight, sums, after=None, bias=None):
    rows, cols, size = xs[0].shape
    outs, _, taps, _, _ = conv_weight.shape
    final = bias is not None
    whole = lambda i, s: (0, 0, 0)
    at_out = lambda i, s: (output_in(s[i]), 0, 0, 0)
    in_channels = lambda n: pl.BlockSpec((n, cols, size), lambda i, s: (0, 0, output_in(s[i])))

    def weights(i, s):
        out, slot = kernel_in(s[i])
        return out, slot, 0, 0, 0

    in_specs = [pl.BlockSpec(memory_space=pl.ANY)] * len(xs) + [
        pl.BlockSpec((len(xs), cols, size), whole),
        pl.BlockSpec((len(xs), cols, size), whole),
        pl.BlockSpec((1, 1, taps, size, size), weights),
        pl.BlockSpec((1, rows, cols, size), at_out),
    ]
    args = [codes, *xs, top, bottom, conv_weight, sums]
    scratch = [pltpu.VMEM((2, rows + 2, cols, size), jnp.bfloat16), pltpu.SemaphoreType.DMA((2,))]
    if final:
        in_specs.append(pl.BlockSpec((1, size), lambda i, s: (0, output_in(s[i]))))
        args.append(bias)
        heights = (rows, 2, 2)
        out_shape = tuple(jax.ShapeDtypeStruct((n, cols, outs * size), jnp.bfloat16) for n in heights)
        out_specs = tuple(in_channels(n) for n in heights)
        scratch.append(pltpu.VMEM((1, rows, cols, size), jnp.float32))
        alias = {}
    else:
        in_specs.append(pl.BlockSpec(memory_space=pl.ANY))
        args.append(after)
        out_shape = jax.ShapeDtypeStruct(sums.shape, sums.dtype)
        out_specs = pl.BlockSpec((1, rows, cols, size), at_out)
        alias = {4 + len(xs): 0}
    return pl.pallas_call(
        functools.partial(more_kernel, final, len(xs)),
        out_shape=out_shape,
        grid_spec=pltpu.PrefetchScalarGridSpec(
            num_scalar_prefetch=1,
            grid=(codes.shape[0],),
            in_specs=in_specs,
            out_specs=out_specs,
            scratch_shapes=scratch,
        ),
        input_output_aliases=alias,
        compiler_params=pltpu.CompilerParams(vmem_limit_bytes=VMEM_BYTES),
        cost_estimate=LIGHT,
        name="last_sums" if final else "more_sums",
    )(*args)


def branch_kernel(x_ref, top_ref, bottom_ref, image_ref, weight_ref, out_ref, xe_ref):
    rows, cols, _ = x_ref.shape
    xe_ref[0:2] = top_ref[...]
    xe_ref[2 : rows + 2] = x_ref[...]
    xe_ref[rows + 2 : rows + 4] = bottom_ref[...]

    def weight_of(c):
        return jnp.concatenate([weight_ref[0, 3 * a + c] for a in range(3)], axis=0)

    def add(r, n, total):
        at = pl.ds(r, n)
        out_ref[at] = (image_ref[at].astype(jnp.float32) + total).astype(out_ref.dtype)

    stencil(xe_ref, weight_of, rows, cols, 2, add)


def branch_out(hidden, top, bottom, image, paired):
    rows, cols, chans = image.shape
    pairs, taps, size, _ = paired.shape
    block = lambda n: pl.BlockSpec((n, cols, size), lambda o: (0, 0, o))
    return pl.pallas_call(
        branch_kernel,
        out_shape=jax.ShapeDtypeStruct(image.shape, image.dtype),
        grid=(pairs,),
        in_specs=[
            block(rows),
            block(2),
            block(2),
            block(rows),
            pl.BlockSpec((1, taps, size, size), lambda o: (o, 0, 0, 0)),
        ],
        out_specs=block(rows),
        scratch_shapes=[pltpu.VMEM((rows + 4, cols, size), jnp.bfloat16)],
        compiler_params=pltpu.CompilerParams(vmem_limit_bytes=VMEM_BYTES),
        cost_estimate=LIGHT,
        name="branch_out",
    )(hidden, top, bottom, image, paired)


def pair_weights(group_weight):
    groups, taps, g, _ = group_weight.shape
    w = group_weight.reshape(groups // 2, 2, taps, g, g)
    upper = jnp.pad(w[:, 0], ((0, 0), (0, 0), (0, g), (0, g)))
    lower = jnp.pad(w[:, 1], ((0, 0), (0, 0), (g, 0), (g, 0)))
    return upper + lower


def along_rows(upper, lower):
    n = lax.axis_size("rows")
    down = [(i, i + 1) for i in range(n - 1)]
    up = [(i + 1, i) for i in range(n - 1)]
    return lax.ppermute(upper, "rows", down), lax.ppermute(lower, "rows", up)


def shards(image, block_links, fan_count, conv_weight, conv_bias, group_weight):
    rows, cols, _ = image.shape
    outs, fan, taps, size, _ = conv_weight.shape
    own = image.shape[2] // size
    blocks = block_links.shape[0]
    chans = lax.axis_size("chan")
    z = lax.axis_index("chan")
    most = most_rounds(chans, own)
    lag = lag_of(own)

    picks, slot_of = make_plan(block_links, fan_count, chans, own, most)
    picks = picks[:, :, 0]
    rounds = jnp.sum(jnp.any(picks >= 0, axis=1).astype(jnp.int32))
    padded = jnp.pad(picks, ((0, 0), (1, 1)), constant_values=-1)
    mirror = chans + chans - 1 - z
    at = lambda r: lax.dynamic_slice_in_dim(padded, r + 1, 1, 1)
    nothing = jnp.full((most, 1), -1, jnp.int32)
    got_left = jnp.where(z > 0, at(z - 1), nothing)
    got_right = jnp.where(z < chans - 1, at(mirror - 1), nothing)
    table = jnp.concatenate([at(z), at(mirror), got_left, got_right], axis=1)
    right = [(i, i + 1) for i in range(chans - 1)]
    left = [(i + 1, i) for i in range(chans - 1)]

    def run(count, table, slot_of, image, conv_weight, conv_bias, group_weight):
        my_slots = lax.dynamic_slice_in_dim(slot_of, z * outs, outs, 0)[:, :blocks]
        own_slots = lax.dynamic_slice_in_dim(my_slots, z * own, own, 1).reshape(1, -1)
        arrived = table[:, 2:]
        hit = arrived[:, None, :, None] == jnp.arange(blocks, dtype=jnp.int32)
        single = jnp.max(jnp.where(hit, my_slots[None, :, None, :], -1), axis=-1)
        even = most + most % 2
        double = jnp.pad(single, ((0, even - most), (0, 0), (0, 0)), constant_values=-1)
        double = double.reshape(even // 2, 2, outs, 2).transpose(0, 2, 1, 3).reshape(even // 2, outs * 4)
        single = single.reshape(most, outs * 2)
        own_steps = every_step(own_slots, own, keep=True)[0]
        double_steps = [compact_steps(double, 4, part, 2) for part in range(2)]
        single_steps = compact_steps(single, 2)
        last_steps = every_step(single, 2)
        me = z.reshape(1)
        table = table.reshape(-1)
        paired = pair_weights(group_weight)
        bias = conv_bias.reshape(1, -1)
        from_left, from_right = [], []
        own_rims = along_rows(image[rows - 1 :], image[:1])
        sums = out_right = None
        waiting = []

        def arrivals(at):
            return [x for k in at for x in (from_left[k], from_right[k])]

        edges = {}

        def work(sums, out_right):
            kind, at = waiting.pop(0)
            if kind == "own":
                half = own_steps.shape[0] // len(own_parts)
                part = own_steps[at * half : (at + 1) * half]
                return own_sums(part, image, *own_rims, conv_weight, out_right, sums)
            if at not in edges:
                edges[at] = along_rows(*rims_of(arrivals(at), out_right if sums is None else sums))
            steps = single_steps[at[0]] if kind == "single" else double_steps[kind][at[0] // 2]
            return more_sums(steps, arrivals(at), *edges[at], conv_weight, sums, out_right)

        own_parts = range(2 if outs % 2 == 0 else 1)
        paired_up = 0
        for k in range(count + 1):
            if k < count:
                ready = max(k - lag + 1, 0)
                out_right, out_left = choose(
                    k, own, size, me, table, image, from_left[:ready], from_right[:ready], [] if sums is None else [sums]
                )
                from_left.append(lax.ppermute(out_right, "chan", right))
                from_right.append(lax.ppermute(out_left, "chan", left))
            if k == 1:
                waiting += [("own", part) for part in own_parts]
            if paired_up + 2 <= min(k - 1, count - 1):
                waiting += [(part, (paired_up, paired_up + 1)) for part in range(2)]
                paired_up += 2
            if waiting and k < count:
                sums = work(sums, out_right)
        waiting += [("single", (k,)) for k in range(paired_up, count - 1)]
        while waiting:
            sums = work(sums, out_right)
        xs = arrivals([count - 1])
        edge = along_rows(*rims_of(xs, sums))
        hidden, head, tail = more_sums(last_steps[count - 1], xs, *edge, conv_weight, sums, bias=bias)
        return branch_out(hidden, *along_rows(tail, head), image, paired)

    choices = list(range(blocks // 2, most + 1)) if chans <= 4 else [most]
    given = (table, slot_of, image, conv_weight, conv_bias, group_weight)
    if len(choices) == 1:
        return run(choices[0], *given)
    branch = jnp.clip(rounds - choices[0], 0, len(choices) - 1)
    return lax.switch(branch, [functools.partial(run, n) for n in choices], *given)


def solution(mesh):
    in_specs = (
        P(("groups", "rows"), None, "chan"),
        P(),
        P(),
        P("chan", None, None, None, None),
        P("chan"),
        P("chan", None, None, None),
    )
    out_specs = P(("groups", "rows"), None, "chan")
    return jax.shard_map(shards, mesh=mesh, in_specs=in_specs, out_specs=out_specs, check_vma=False)
```

```python
import functools

import jax
import jax.numpy as jnp
from jax import lax
from jax.experimental import pallas as pl
from jax.experimental.pallas import tpu as pltpu
from jax.sharding import PartitionSpec as P

LANES = 128
VMEM_BYTES = 48 << 20


def lag_of(own):
    return 2 if own >= 2 else 1


def most_rounds(chans, own):
    lag = lag_of(own)
    return max(hop * lag + (chans - 1 - hop) * own for hop in range(chans - 1))


def plan_kernel(chans, own, rounds, links_ref, fans_ref, pick_ref, slot_ref):
    blocks, fan = links_ref.shape
    lag = lag_of(own)
    lane = lax.broadcasted_iota(jnp.int32, (blocks, LANES), 1)
    links = links_ref[...]
    fans = fans_ref[...]
    slot = jnp.full((blocks, LANES), -1, jnp.int32)
    for s in range(fan):
        slot = jnp.where((links[:, s : s + 1] == lane) & (fans > s), s, slot)
    slot_ref[...] = slot
    used = jnp.where(slot >= 0, 1.0, 0.0)
    far = jnp.full((1, LANES), -1.0, jnp.float32)
    near = jnp.full((1, LANES), float(chans), jnp.float32)
    for z in range(chans):
        up = jnp.max(used[z * own : (z + 1) * own], axis=0, keepdims=True)
        far = jnp.where(up > 0, float(z), far)
        w = chans - 1 - z
        down = jnp.max(used[w * own : (w + 1) * own], axis=0, keepdims=True)
        near = jnp.where(down > 0, float(w), near)
    shape = (2 * chans, LANES)
    row = lax.broadcasted_iota(jnp.int32, shape, 0)
    block = lax.broadcasted_iota(jnp.int32, shape, 1)
    mirrored = row >= chans
    here = jnp.where(mirrored, row - chans, row).astype(jnp.float32)
    home = jnp.zeros(shape, jnp.float32)
    for z in range(1, chans):
        home = home + jnp.where(block >= z * own, 1.0, 0.0)
    home = jnp.where(mirrored, chans - 1.0 - home, home)
    reach = jnp.where(mirrored, chans - 1.0 - near, far)
    blockf = block.astype(jnp.float32)
    left = jnp.where((reach > here) & (home <= here) & (block < blocks), 1.0, 0.0)
    held = jnp.where(home == here, 1.0, 0.0)
    rank = reach * 4096.0 + home * 128.0 + blockf
    sent = []
    for k in range(rounds):
        if k >= lag:
            held = jnp.maximum(held, pltpu.roll(sent[k - lag], 1, 0))
        score = jnp.where((left > 0) & (held > 0), rank, -1.0)
        best = jnp.max(score, axis=1, keepdims=True)
        chosen = jnp.where((score == best) & (best >= 0), 1.0, 0.0)
        sent.append(chosen)
        left = left - chosen
        which = jnp.max(jnp.where(chosen > 0, blockf, -1.0), axis=1, keepdims=True)
        pick_ref[k] = jnp.broadcast_to(which, shape).astype(jnp.int32)


def make_plan(block_links, fan_count, chans, own, rounds):
    blocks = block_links.shape[0]
    return pl.pallas_call(
        functools.partial(plan_kernel, chans, own, rounds),
        out_shape=(
            jax.ShapeDtypeStruct((rounds, 2 * chans, LANES), jnp.int32),
            jax.ShapeDtypeStruct((blocks, LANES), jnp.int32),
        ),
        name="plan",
    )(block_links, fan_count.reshape(blocks, 1))


def quarters(rows):
    step = rows // 4
    return [pl.ds(i * step, step) for i in range(4)]


def choose_kernel(k, own, size, held, me_ref, table_ref, image_ref, *refs):
    from_left, from_right = refs[:held], refs[held : 2 * held]
    right_ref, left_ref, sems = refs[-3:]
    base = me_ref[0] * own
    for d, (out_ref, got) in enumerate(((right_ref, from_left), (left_ref, from_right))):
        block = table_ref[4 * k + d]
        mine = (block >= base) & (block < base + own)

        @pl.when(mine)
        def _(d=d, out_ref=out_ref, block=block):
            start = pl.multiple_of((block - base) * size, size)
            for at in quarters(out_ref.shape[0]):
                pltpu.make_async_copy(image_ref.at[at, :, pl.ds(start, size)], out_ref.at[at], sems.at[d]).start()

        for j in range(held):
            same = (block >= 0) & jnp.logical_not(mine) & (table_ref[4 * j + 2 + d] == block)

            @pl.when(same)
            def _(d=d, out_ref=out_ref, ref=got[j]):
                for at in quarters(out_ref.shape[0]):
                    pltpu.make_async_copy(ref.at[at], out_ref.at[at], sems.at[d]).start()

    for d, out_ref in enumerate((right_ref, left_ref)):

        @pl.when(table_ref[4 * k + d] >= 0)
        def _(d=d, out_ref=out_ref):
            pltpu.make_async_copy(image_ref.at[:, :, pl.ds(0, size)], out_ref, sems.at[d]).wait()


def choose(k, own, size, me, table, image, from_left, from_right, after):
    rows, cols, _ = image.shape
    shape = jax.ShapeDtypeStruct((rows, cols, size), image.dtype)
    anywhere = pl.BlockSpec(memory_space=pl.ANY)
    scalars = pl.BlockSpec(memory_space=pltpu.SMEM)
    return pl.pallas_call(
        functools.partial(choose_kernel, k, own, size, len(from_left)),
        out_shape=(shape, shape),
        in_specs=[scalars, scalars] + [anywhere] * (1 + len(from_left) + len(from_right) + len(after)),
        out_specs=(pl.BlockSpec(memory_space=pltpu.VMEM),) * 2,
        scratch_shapes=[pltpu.SemaphoreType.DMA((2,))],
        compiler_params=pltpu.CompilerParams(vmem_limit_bytes=VMEM_BYTES),
        cost_estimate=pl.CostEstimate(flops=0, bytes_accessed=4 * rows * cols * size * 2, transcendentals=0),
        name=f"choose_{k}",
    )(me, table, image, *from_left, *from_right, *after)


def shifted(y, step, col):
    cols = y.shape[1]
    moved = pltpu.roll(y, step % cols, 1)
    return jnp.where((col >= step) & (col < cols + step), moved, 0.0)


def stencil(xe_ref, weight_of, rows, cols, gap, add):
    step = 4
    width = xe_ref.shape[2]
    col = lax.broadcasted_iota(jnp.int32, (step, cols, 1), 1)

    def few(i, carry):
        r = i * step
        wide = jnp.concatenate(
            [xe_ref[pl.ds(r + a * gap, step)].reshape(step * cols, width) for a in range(3)], axis=1
        )
        total = None
        for c in range(3):
            y = jnp.dot(wide, weight_of(c), preferred_element_type=jnp.float32)
            y = y.reshape(step, cols, y.shape[-1])
            if c != 1:
                y = shifted(y, (1 - c) * gap, col)
            total = y if total is None else total + y
        add(r, step, total)
        return carry

    lax.fori_loop(0, rows // step, few, 0, unroll=True)


def source_in(code):
    return (code >> 2) & 63


def output_in(code):
    return (code >> 8) & 255


def kernel_in(code):
    return (code >> 16) & 255, code >> 24


def compact_steps(slots, sources, part=0, parts=1):
    count = slots.shape[1]
    valid = slots >= 0
    index = jnp.arange(count, dtype=jnp.int32)
    place = jnp.sum(jnp.where(valid[:, None, :] & (index[None, :] < index[:, None])[None], 1, 0), axis=2)
    total = jnp.sum(valid.astype(jnp.int32), axis=1, keepdims=True)
    skipped = jnp.zeros_like(total)
    step = index
    if parts == 2:
        half = (total + 1) >> 1
        skipped, total = (half, total - half) if part else (skipped, half)
        step = index[: (count + 1) // 2]
    want = skipped + jnp.minimum(step[None, :], jnp.maximum(total - 1, 0))
    pick = valid[:, None, :] & (place[:, None, :] == want[:, :, None])
    take = lambda v: jnp.sum(jnp.where(pick, v, 0), axis=2)
    entry = take(index[None, None, :])
    out = entry // sources
    slot = take(slots[:, None, :])
    active = (step[None, :] < total).astype(jnp.int32)
    before = jnp.concatenate([jnp.full_like(out[:, :1], -1), out[:, :-1]], axis=1)
    first = (out != before).astype(jnp.int32)
    return active | (first << 1) | ((entry % sources) << 2) | (out << 8) | (out << 16) | (slot << 24)


def every_step(slots, sources, keep=False):
    count = slots.shape[1]
    valid = slots >= 0
    index = jnp.arange(count, dtype=jnp.int32)
    up_to = (index[None, :] <= index[:, None])[None]
    latest = jnp.max(jnp.where(valid[:, None, :] & up_to, index[None, None, :], -1), axis=2)
    soonest = jnp.min(jnp.where(valid, index[None, :], count - 1), axis=1, keepdims=True)
    entry = jnp.where(latest >= 0, latest, soonest)
    pick = entry[:, :, None] == index[None, None, :]
    slot = jnp.maximum(jnp.sum(jnp.where(pick, slots[:, None, :], 0), axis=2), 0)
    first = (index % sources == 0).astype(jnp.int32)
    source = entry % sources if keep else (index % sources)[None]
    fixed = (first << 1) | ((index // sources) << 8)
    return valid.astype(jnp.int32) | fixed[None] | (source << 2) | ((entry // sources) << 16) | (slot << 24)


def fill(xe_ref, x_ref, top, bottom):
    rows = x_ref.shape[0]
    xe_ref[1 : rows + 1] = x_ref[...]
    xe_ref[0:1] = top
    xe_ref[rows + 1 : rows + 2] = bottom


def add_block(xe_ref, weight_ref, sums_ref):
    _, rows, cols, _ = sums_ref.shape

    def weight_of(c):
        return jnp.concatenate([weight_ref[0, 0, 3 * a + c] for a in range(3)], axis=0)

    def add(r, n, total):
        sums_ref[0, pl.ds(r, n)] += total

    stencil(xe_ref, weight_of, rows, cols, 1, add)


def rims_kernel(count, *refs):
    xs, (last_ref, first_ref, sems) = refs[:count], refs[-3:]
    copies = []
    for i, x_ref in enumerate(xs):
        rows = x_ref.shape[0]
        for d, (row, out_ref) in enumerate(((rows - 1, last_ref), (0, first_ref))):
            copies.append(
                pltpu.make_async_copy(x_ref.at[pl.ds(row, 1)], out_ref.at[pl.ds(i, 1)], sems.at[d, i])
            )
    for copy in copies:
        copy.start()
    for copy in copies:
        copy.wait()


def rims_of(xs, after):
    _, cols, size = xs[0].shape
    shape = jax.ShapeDtypeStruct((len(xs), cols, size), xs[0].dtype)
    return pl.pallas_call(
        functools.partial(rims_kernel, len(xs)),
        out_shape=(shape, shape),
        in_specs=[pl.BlockSpec(memory_space=pl.ANY)] * (len(xs) + 1),
        out_specs=(pl.BlockSpec(memory_space=pltpu.VMEM),) * 2,
        scratch_shapes=[pltpu.SemaphoreType.DMA((2, len(xs)))],
        compiler_params=pltpu.CompilerParams(vmem_limit_bytes=VMEM_BYTES),
        cost_estimate=LIGHT,
        name="rims",
    )(*xs, after)


LIGHT = pl.CostEstimate(flops=0, bytes_accessed=1 << 20, transcendentals=0)


def own_kernel(codes_ref, x_ref, top_ref, bottom_ref, weight_ref, *refs):
    sums_ref, xe_ref = refs[-2:]
    code = codes_ref[pl.program_id(0)]

    @pl.when((code & 2) > 0)
    def _():
        sums_ref[...] = jnp.zeros_like(sums_ref)

    @pl.when((code & 1) > 0)
    def _():
        fill(xe_ref, x_ref, top_ref[...], bottom_ref[...])
        add_block(xe_ref, weight_ref, sums_ref)


def own_sums(codes, image, top, bottom, conv_weight, after, before=None):
    rows, cols, _ = image.shape
    outs, _, taps, size, _ = conv_weight.shape
    source = lambda i, s: (0, 0, source_in(s[i]))
    extra = [after] if before is None else [after, before]

    def weights(i, s):
        out, slot = kernel_in(s[i])
        return out, slot, 0, 0, 0

    return pl.pallas_call(
        own_kernel,
        out_shape=jax.ShapeDtypeStruct((outs, rows, cols, size), jnp.float32),
        grid_spec=pltpu.PrefetchScalarGridSpec(
            num_scalar_prefetch=1,
            grid=(codes.shape[0],),
            in_specs=[
                pl.BlockSpec((rows, cols, size), source),
                pl.BlockSpec((1, cols, size), source),
                pl.BlockSpec((1, cols, size), source),
                pl.BlockSpec((1, 1, taps, size, size), weights),
            ]
            + [pl.BlockSpec(memory_space=pl.ANY)] * len(extra),
            out_specs=pl.BlockSpec((1, rows, cols, size), lambda i, s: (output_in(s[i]), 0, 0, 0)),
            scratch_shapes=[pltpu.VMEM((rows + 2, cols, size), jnp.bfloat16)],
        ),
        compiler_params=pltpu.CompilerParams(vmem_limit_bytes=VMEM_BYTES),
        input_output_aliases={} if before is None else {6: 0},
        cost_estimate=LIGHT,
        name="own_sums",
    )(codes, image, top, bottom, conv_weight, *extra)


def more_kernel(final, count, codes_ref, *refs):
    xs, refs = refs[:count], refs[count:]
    top_ref, bottom_ref, weight_ref, before_ref = refs[:4]
    if final:
        bias_ref, out_ref, head_ref, tail_ref, xe_ref, sems, sums_ref = refs[4:]
    else:
        _, sums_ref, xe_ref, sems = refs[4:]
    step, steps = pl.program_id(0), codes_ref.shape[0]
    code = codes_ref[step]
    now = lax.rem(step, 2)
    rows = xs[0].shape[0]

    def fetch(code, slot):
        for side, x_ref in enumerate(xs):

            @pl.when(((code & 1) > 0) & (source_in(code) == side))
            def _(x_ref=x_ref):
                for at in quarters(rows):
                    into = xe_ref.at[slot, pl.ds(at.start + 1, at.size)]
                    pltpu.make_async_copy(x_ref.at[at], into, sems.at[slot]).start()

    @pl.when(step == 0)
    def _():
        fetch(code, 0)

    @pl.when(step + 1 < steps)
    def _():
        fetch(codes_ref[jnp.minimum(step + 1, steps - 1)], 1 - now)

    @pl.when((code & 2) > 0)
    def _():
        sums_ref[...] = before_ref[...]

    @pl.when((code & 1) > 0)
    def _():
        side = source_in(code)
        xe_ref[now, 0] = top_ref[side]
        xe_ref[now, rows + 1] = bottom_ref[side]
        pltpu.make_async_copy(xs[0], xe_ref.at[now, pl.ds(1, rows)], sems.at[now]).wait()
        add_block(xe_ref.at[now], weight_ref, sums_ref)

    if final:

        @pl.when(source_in(code) == count - 1)
        def _():
            out = jnp.maximum(sums_ref[0] + bias_ref[...].reshape(1, 1, -1), 0.0).astype(out_ref.dtype)
            out_ref[...] = out
            head_ref[...] = out[:2]
            tail_ref[...] = out[rows - 2 :]


def more_sums(codes, xs, top, bottom, conv_weight, sums, after=None, bias=None):
    rows, cols, size = xs[0].shape
    outs, _, taps, _, _ = conv_weight.shape
    final = bias is not None
    whole = lambda i, s: (0, 0, 0)
    at_out = lambda i, s: (output_in(s[i]), 0, 0, 0)
    in_channels = lambda n: pl.BlockSpec((n, cols, size), lambda i, s: (0, 0, output_in(s[i])))

    def weights(i, s):
        out, slot = kernel_in(s[i])
        return out, slot, 0, 0, 0

    in_specs = [pl.BlockSpec(memory_space=pl.ANY)] * len(xs) + [
        pl.BlockSpec((len(xs), cols, size), whole),
        pl.BlockSpec((len(xs), cols, size), whole),
        pl.BlockSpec((1, 1, taps, size, size), weights),
        pl.BlockSpec((1, rows, cols, size), at_out),
    ]
    args = [codes, *xs, top, bottom, conv_weight, sums]
    scratch = [pltpu.VMEM((2, rows + 2, cols, size), jnp.bfloat16), pltpu.SemaphoreType.DMA((2,))]
    if final:
        in_specs.append(pl.BlockSpec((1, size), lambda i, s: (0, output_in(s[i]))))
        args.append(bias)
        heights = (rows, 2, 2)
        out_shape = tuple(jax.ShapeDtypeStruct((n, cols, outs * size), jnp.bfloat16) for n in heights)
        out_specs = tuple(in_channels(n) for n in heights)
        scratch.append(pltpu.VMEM((1, rows, cols, size), jnp.float32))
        alias = {}
    else:
        in_specs.append(pl.BlockSpec(memory_space=pl.ANY))
        args.append(after)
        out_shape = jax.ShapeDtypeStruct(sums.shape, sums.dtype)
        out_specs = pl.BlockSpec((1, rows, cols, size), at_out)
        alias = {4 + len(xs): 0}
    return pl.pallas_call(
        functools.partial(more_kernel, final, len(xs)),
        out_shape=out_shape,
        grid_spec=pltpu.PrefetchScalarGridSpec(
            num_scalar_prefetch=1,
            grid=(codes.shape[0],),
            in_specs=in_specs,
            out_specs=out_specs,
            scratch_shapes=scratch,
        ),
        input_output_aliases=alias,
        compiler_params=pltpu.CompilerParams(vmem_limit_bytes=VMEM_BYTES),
        cost_estimate=LIGHT,
        name="last_sums" if final else "more_sums",
    )(*args)


def branch_kernel(x_ref, top_ref, bottom_ref, image_ref, group_ref, out_ref, xe_ref, weight_ref):
    rows, cols, _ = x_ref.shape
    g = group_ref.shape[-1]

    @pl.when(pl.program_id(0) == 0)
    def _():
        weight_ref[...] = jnp.zeros_like(weight_ref)

    weight_ref[:, :g, :g] = group_ref[0]
    weight_ref[:, g:, g:] = group_ref[1]
    xe_ref[0:2] = top_ref[...]
    xe_ref[2 : rows + 2] = x_ref[...]
    xe_ref[rows + 2 : rows + 4] = bottom_ref[...]

    def weight_of(c):
        return jnp.concatenate([weight_ref[3 * a + c] for a in range(3)], axis=0)

    def add(r, n, total):
        at = pl.ds(r, n)
        out_ref[at] = (image_ref[at].astype(jnp.float32) + total).astype(out_ref.dtype)

    stencil(xe_ref, weight_of, rows, cols, 2, add)


def branch_out(hidden, top, bottom, image, group_weight):
    rows, cols, chans = image.shape
    groups, taps, g, _ = group_weight.shape
    size = 2 * g
    block = lambda n: pl.BlockSpec((n, cols, size), lambda o: (0, 0, o))
    return pl.pallas_call(
        branch_kernel,
        out_shape=jax.ShapeDtypeStruct(image.shape, image.dtype),
        grid=(groups // 2,),
        in_specs=[
            block(rows),
            block(2),
            block(2),
            block(rows),
            pl.BlockSpec((2, taps, g, g), lambda o: (o, 0, 0, 0)),
        ],
        out_specs=block(rows),
        scratch_shapes=[
            pltpu.VMEM((rows + 4, cols, size), jnp.bfloat16),
            pltpu.VMEM((taps, size, size), jnp.bfloat16),
        ],
        compiler_params=pltpu.CompilerParams(vmem_limit_bytes=VMEM_BYTES),
        cost_estimate=LIGHT,
        name="branch_out",
    )(hidden, top, bottom, image, group_weight)


def along_rows(upper, lower):
    n = lax.axis_size("rows")
    down = [(i, i + 1) for i in range(n - 1)]
    up = [(i + 1, i) for i in range(n - 1)]
    return lax.ppermute(upper, "rows", down), lax.ppermute(lower, "rows", up)


def shards(image, block_links, fan_count, conv_weight, conv_bias, group_weight):
    rows, cols, _ = image.shape
    outs, fan, taps, size, _ = conv_weight.shape
    own = image.shape[2] // size
    blocks = block_links.shape[0]
    chans = lax.axis_size("chan")
    z = lax.axis_index("chan")
    most = most_rounds(chans, own)
    lag = lag_of(own)

    picks, slot_of = make_plan(block_links, fan_count, chans, own, most)
    picks = picks[:, :, 0]
    rounds = jnp.sum(jnp.any(picks >= 0, axis=1).astype(jnp.int32))
    padded = jnp.pad(picks, ((0, 0), (1, 1)), constant_values=-1)
    mirror = chans + chans - 1 - z
    at = lambda r: lax.dynamic_slice_in_dim(padded, r + 1, 1, 1)
    nothing = jnp.full((most, 1), -1, jnp.int32)
    got_left = jnp.where(z > 0, at(z - 1), nothing)
    got_right = jnp.where(z < chans - 1, at(mirror - 1), nothing)
    table = jnp.concatenate([at(z), at(mirror), got_left, got_right], axis=1)
    right = [(i, i + 1) for i in range(chans - 1)]
    left = [(i + 1, i) for i in range(chans - 1)]

    def run(count, table, slot_of, image, conv_weight, conv_bias, group_weight):
        my_slots = lax.dynamic_slice_in_dim(slot_of, z * outs, outs, 0)[:, :blocks]
        own_slots = lax.dynamic_slice_in_dim(my_slots, z * own, own, 1).reshape(1, -1)
        arrived = table[:, 2:]
        hit = arrived[:, None, :, None] == jnp.arange(blocks, dtype=jnp.int32)
        single = jnp.max(jnp.where(hit, my_slots[None, :, None, :], -1), axis=-1)
        even = most + most % 2
        double = jnp.pad(single, ((0, even - most), (0, 0), (0, 0)), constant_values=-1)
        double = double.reshape(even // 2, 2, outs, 2).transpose(0, 2, 1, 3).reshape(even // 2, outs * 4)
        single = single.reshape(most, outs * 2)
        own_steps = every_step(own_slots, own, keep=True)[0]
        double_steps = [compact_steps(double, 4, part, 2) for part in range(2)]
        single_steps = compact_steps(single, 2)
        last_steps = every_step(single, 2)
        me = z.reshape(1)
        table = table.reshape(-1)
        bias = conv_bias.reshape(1, -1)
        from_left, from_right = [], []
        own_rims = along_rows(image[rows - 1 :], image[:1])
        sums = out_right = None
        waiting = []

        def arrivals(at):
            return [x for k in at for x in (from_left[k], from_right[k])]

        edges = {}

        def work(sums, out_right):
            kind, at = waiting.pop(0)
            if kind == "own":
                half = own_steps.shape[0] // len(own_parts)
                part = own_steps[at * half : (at + 1) * half]
                return own_sums(part, image, *own_rims, conv_weight, out_right, sums)
            if at not in edges:
                edges[at] = along_rows(*rims_of(arrivals(at), out_right if sums is None else sums))
            steps = single_steps[at[0]] if kind == "single" else double_steps[kind][at[0] // 2]
            return more_sums(steps, arrivals(at), *edges[at], conv_weight, sums, out_right)

        own_parts = range(2 if outs % 2 == 0 else 1)
        paired_up = 0
        for k in range(count + 1):
            if k < count:
                ready = max(k - lag + 1, 0)
                out_right, out_left = choose(
                    k, own, size, me, table, image, from_left[:ready], from_right[:ready], [x for x in (sums, out_right) if x is not None][:1]
                )
                from_left.append(lax.ppermute(out_right, "chan", right))
                from_right.append(lax.ppermute(out_left, "chan", left))
            if k == 1:
                waiting += [("own", part) for part in own_parts]
            if paired_up + 2 <= min(k - 1, count - 1):
                waiting += [(part, (paired_up, paired_up + 1)) for part in range(2)]
                paired_up += 2
            if waiting and k < count:
                sums = work(sums, out_right)
        waiting += [("single", (k,)) for k in range(paired_up, count - 1)]
        while waiting:
            sums = work(sums, out_right)
        xs = arrivals([count - 1])
        edge = along_rows(*rims_of(xs, sums))
        hidden, head, tail = more_sums(last_steps[count - 1], xs, *edge, conv_weight, sums, bias=bias)
        return branch_out(hidden, *along_rows(tail, head), image, group_weight)

    choices = list(range(blocks // 2, most + 1)) if chans <= 4 else [most]
    given = (table, slot_of, image, conv_weight, conv_bias, group_weight)
    if len(choices) == 1:
        return run(choices[0], *given)
    branch = jnp.clip(rounds - choices[0], 0, len(choices) - 1)
    return lax.switch(branch, [functools.partial(run, n) for n in choices], *given)


def solution(mesh):
    in_specs = (
        P(("groups", "rows"), None, "chan"),
        P(),
        P(),
        P("chan", None, None, None, None),
        P("chan"),
        P("chan", None, None, None),
    )
    out_specs = P(("groups", "rows"), None, "chan")
    return jax.shard_map(shards, mesh=mesh, in_specs=in_specs, out_specs=out_specs, check_vma=False)
```
